256 devices in a mesh: replica: 8 (over z_lo, core), fsdp: 32 (over z_hi, x, y).
Axes of the slice: x: 4, y: 4, z: 8 (z_hi: 2, z_lo: 4; z = z_hi * 4 + z_lo), core: 2. Of those that a mesh axis runs over, the one named last changes fastest.
Arguments:
- anchor: float32 [8192, 1024], P('fsdp'), may hold values from -6 to 6
- first_moment: float32 [8, 8192, 1024], P('replica', 'fsdp'), may hold values from -4 to 4
- second_moment: float32 [8, 8192, 1024], P('replica', 'fsdp'), may hold values from 0.3 to 3
- outer_momentum: float32 [8192, 1024], P('fsdp'), may hold values from -6 to 6
- activations: bfloat16 [8, 2, 4096, 8192], P('replica', None, 'fsdp'), may hold values from -6 to 6
- cotangents: bfloat16 [8, 2, 4096, 1024], P('replica', None, 'fsdp'), may hold values from -0.21875 to 0.21875
- token_ids: int32 [8, 2, 4096], P('replica', None, 'fsdp'), may hold values from 0 to 128255, as said below
- exponents: int32 [8, 8192, 8], P('replica', 'fsdp'), may hold values from -13 to -9
Outputs:
- new_weights: float32 [8192, 1024], P('fsdp')
- new_momentum: float32 [8192, 1024], P('fsdp')
- new_first: float32 [8, 8192, 1024], P('replica', 'fsdp')
- new_second: float32 [8, 8192, 1024], P('replica', 'fsdp')
The draws below stay inside these ranges and needn't reach their ends.
Inputs may be any that keep to these rules, and one draw needn't show every extreme that they name: `token_ids`: 0 is the padding id; in each aligned block of 128 tokens of one replica and step the padding is a tail, and the first quarter of the block or more is not padding.
All inputs are finite; a program needn't handle non-finite values.
Results may differ from the reference program's by a relative error of at most 0.0055.
Values may be sent and summed in bfloat16 or wider, within the bound.
No kernel may reach another device: no remote copies, remote signals or barrier semaphores. Data moves between devices by JAX's collectives and lax.ppermute only.
A program may use at most 192 MiB of HBM per device.

```python
import math
import jax
import jax.numpy as jnp
from jax import lax

D = 8192
C = 1024
VOCAB = 128256
INNER = 2
TOK_DEV = 128
TOKENS = 4096
REPLICAS = 8


def draw_token_ids(key, part):
    key = jax.random.fold_in(key, 7)
    key_ids, key_live = jax.random.split(key)
    blocks = TOKENS // TOK_DEV
    identity = jax.random.randint(key_ids, (REPLICAS, INNER, TOKENS), 1, VOCAB)
    live = jax.random.randint(key_live, (REPLICAS, INNER, blocks), TOK_DEV // 4, TOK_DEV + 1)
    position = jnp.arange(TOKENS, dtype=jnp.int32)
    offset = position % TOK_DEV
    owner = position // TOK_DEV
    keep = offset[None, None, :] < live[:, :, owner]
    return jnp.where(keep, identity, 0).astype(jnp.int32)


def set_ends(entries, own_key, low, top_value):
    spot = [jax.random.randint(jax.random.fold_in(own_key, axis), (), 0, length) for axis, length in enumerate(entries.shape)]
    main_axis = entries.shape.index(max(entries.shape))
    neighbour = spot[:main_axis] + [(spot[main_axis] + 1) % entries.shape[main_axis]] + spot[main_axis + 1:]
    return entries.at[tuple(spot)].set(low).at[tuple(neighbour)].set(top_value)


def shard_levels(own_key, extent, pieces, least, largest):
    def one(axis_at, parts):
        draws = jax.random.uniform(jax.random.fold_in(jax.random.fold_in(own_key, 6), axis_at), (parts,), jnp.float32, least / len(pieces), largest / len(pieces))
        return jnp.repeat(jnp.exp(draws), extent[axis_at] // parts).reshape((-1,) + (1,) * (len(extent) - axis_at - 1))

    factor_of = one(*pieces[0])
    for cut in pieces[1:]:
        factor_of = factor_of * one(*cut)
    return factor_of


def centred(key, dims, scale, limit, pieces=(), kind=jnp.bfloat16):
    array = scale * jax.random.normal(key, dims, jnp.float32)
    if pieces:
        array = array * shard_levels(key, dims, pieces, -0.22, 0.18)
    return jnp.clip(array, -limit, limit).astype(kind)


def setup_inputs(seed: int = 0) -> dict:
    streams_of = jax.random.split(jax.random.key(seed), 9)
    return {
        "anchor": centred(streams_of[0], (D, C), 1.0, 6.0, ((0, 32),), jnp.float32),
        "first_moment": centred(streams_of[1], (REPLICAS, D, C), 0.3, 4.0, ((0, 8), (1, 32)), jnp.float32),
        "second_moment": jnp.clip(jnp.exp(math.log(3.0) - 2.3025851 * jax.random.uniform(streams_of[2], (REPLICAS, D, C), jnp.float32) ** shard_levels(streams_of[2], (REPLICAS, D, C), ((0, 8), (1, 32)), -0.2, 0.2)), 0.3, 3.0),
        "outer_momentum": centred(streams_of[3], (D, C), 0.5, 6.0, ((0, 32),), jnp.float32),
        "activations": centred(streams_of[4], (REPLICAS, INNER, TOKENS, D), 1.0, 6.0, ((0, 8), (2, 32))),
        "cotangents": centred(streams_of[5], (REPLICAS, INNER, TOKENS, C), 0.015, 0.21875, ((0, 8), (2, 32))),
        "token_ids": draw_token_ids(jax.random.fold_in(streams_of[8], 71), 0),
        "exponents": set_ends(jax.random.randint(streams_of[7], (REPLICAS, D, C // 128), -13, -8), jax.random.fold_in(streams_of[7], 1), -13, (-8) - 1).astype(jnp.int32),
    }


BETA_ONE = 0.9
BETA_TWO = 0.95
EPSILON = 1e-08
INNER_RATE = 0.1
DECAY = 0.1
OUTER_RATE = 0.7
MOMENTUM = 0.9
CODE_LIMIT = 448.0

def adam_update(weights, first, second, gradient):
    first = BETA_ONE * first + (1.0 - BETA_ONE) * gradient
    second = BETA_TWO * second + (1.0 - BETA_TWO) * gradient * gradient
    weights = weights - INNER_RATE * (first / (jnp.sqrt(second) + EPSILON) + DECAY * weights)
    return (weights, first, second)

def block_factor(exponents):
    return jnp.left_shift(jnp.ones_like(exponents), -exponents).astype(jnp.float32)

def decode_blocks(delta, exponents):
    blocks = delta.reshape(delta.shape[0], -1, 128)
    factor = block_factor(exponents)[..., None]
    coded = jnp.clip(blocks * factor, -CODE_LIMIT, CODE_LIMIT).astype(jnp.bfloat16)
    coded = lax.optimization_barrier(coded)
    return (coded.astype(jnp.float32) / factor).reshape(delta.shape)

def reference(anchor, first_moment, second_moment, outer_momentum, activations, cotangents, token_ids, exponents):

    def one_replica(item):
        first, second, features, cots, identity, scales = item
        weights = anchor
        for step in range(INNER):
            masked = jnp.where((identity[step] != 0)[:, None], cots[step], jnp.zeros_like(cots[step]))
            gradient = lax.dot_general(features[step], masked, (((0,), (0,)), ((), ())), preferred_element_type=jnp.float32)
            weights, first, second = adam_update(weights, first, second, gradient)
        return (decode_blocks(anchor - weights, scales), first, second)
    decoded, new_first, new_second = lax.map(one_replica, (first_moment, second_moment, activations, cotangents, token_ids, exponents))
    average = lax.optimization_barrier(jnp.sum(decoded, axis=0)) / REPLICAS
    new_momentum = MOMENTUM * outer_momentum + average
    new_weights = anchor - OUTER_RATE * (average + MOMENTUM * new_momentum)
    return (new_weights, new_momentum, new_first, new_second)
```

```python
import functools

import jax
import jax.numpy as jnp
from jax import lax
from jax.experimental import pallas as pl
from jax.experimental.pallas import tpu as pltpu
from jax.sharding import PartitionSpec as P

BETA_ONE = 0.9
BETA_TWO = 0.95
EPSILON = 1e-08
INNER_RATE = 0.1
DECAY = 0.1
OUTER_RATE = 0.7
MOMENTUM = 0.9
CODE_LIMIT = 448.0

NZ, NX, NY = 2, 4, 4
PLANE = NX * NY
LINE, CORES = 4, 2
VMEM = 56 * 1024 * 1024


def fsdp_shift(dz, dx, dy):
    def at(z, x, y):
        return ((z % NZ) * NX + x % NX) * NY + y % NY

    return [
        (at(z, x, y), at(z + dz, x + dx, y + dy))
        for z in range(NZ)
        for x in range(NX)
        for y in range(NY)
    ]


def replica_shift(dz, dc):
    return [
        (z * CORES + c, ((z + dz) % LINE) * CORES + (c + dc) % CORES)
        for z in range(LINE)
        for c in range(CORES)
    ]


PLANES = [list(range(z * PLANE, (z + 1) * PLANE)) for z in range(NZ)]
X_RING = (fsdp_shift(0, 1, 0), fsdp_shift(0, -1, 0))
Y_RING = (fsdp_shift(0, 0, 1), fsdp_shift(0, 0, -1))
Z_SWAP = fsdp_shift(1, 0, 0)


def split_kernel(spot, features, out):
    for q in range(out.shape[0]):
        out[q] = features[0, 0, :, q * 256 : (q + 1) * 256]


def split_rows(spot, features, step):
    tokens, rows = features.shape[2:]
    shard = rows // (NZ * PLANE)
    return pl.pallas_call(
        split_kernel,
        grid_spec=pltpu.PrefetchScalarGridSpec(
            num_scalar_prefetch=1,
            grid=(4,),
            in_specs=[
                pl.BlockSpec((1, 1, tokens, 4 * shard), lambda i, spot: (0, step, 0, spot[0] * 4 + i))
            ],
            out_specs=pl.BlockSpec((4, tokens, shard), lambda i, spot: (i, 0, 0)),
        ),
        out_shape=jax.ShapeDtypeStruct((PLANE, tokens, shard), features.dtype),
    )(spot, features)


def ring_gather(block, ring):
    ahead, back = ring
    left = lax.ppermute(block, "fsdp", ahead)
    right = lax.ppermute(block, "fsdp", back)
    far_zero = lax.ppermute(left[0], "fsdp", ahead)
    far_one = lax.ppermute(right[1], "fsdp", back)
    return block, left, right, (far_zero, far_one)


def stack_pieces(pieces, at):
    own, left, right, (far_zero, far_one) = pieces
    far = jnp.stack([far_zero, far_one])
    whole = jnp.stack([own, left, far, right], axis=1)
    order = lax.rem(at - jnp.arange(4, dtype=jnp.int32) + 4, 4)
    return jnp.take(whole, order, axis=1)


def dot_kernel(step, spot, a, *refs):
    first_set, second_set = refs[0:4], refs[4:8]
    out, tokens, sems = refs[8:]
    x, y = spot[0], spot[1]
    copies = []
    for turn, piece in enumerate(first_set):
        source = piece.at[step] if len(piece.shape) == 4 else piece
        copies.append(
            pltpu.make_async_copy(source, tokens.at[:, lax.rem(y - turn + 4, 4), 0], sems.at[turn])
        )
    for turn, piece in enumerate(second_set):
        source = piece.at[step] if len(piece.shape) == 4 else piece
        copies.append(
            pltpu.make_async_copy(source, tokens.at[lax.rem(x - turn + 4, 4), :, 1], sems.at[4 + turn])
        )
    for copy in copies:
        copy.start()
    left = a[...].reshape(-1, a.shape[-1])
    for copy in copies:
        copy.wait()
    depth = left.shape[0]

    width = 256
    for n in range(0, out.shape[1], width):
        right = tokens[:, :, :, :, n : n + width].reshape(depth, width)
        out[:, n : n + width] = lax.dot_general(
            left, right, (((0,), (0,)), ((), ())), preferred_element_type=jnp.float32
        ).astype(out.dtype)


def contract(spot, a, sets, step, dtype):
    width = sets[0][0].shape[-1]
    pieces = []
    for own, left, right, far in sets:
        pieces += [own, left, far[step], right]
    return pl.pallas_call(
        functools.partial(dot_kernel, step),
        in_specs=[pl.BlockSpec(memory_space=pltpu.SMEM), pl.BlockSpec(memory_space=pltpu.VMEM)]
        + [pl.BlockSpec(memory_space=pl.ANY)] * 8,
        out_specs=pl.BlockSpec(memory_space=pltpu.VMEM),
        out_shape=jax.ShapeDtypeStruct((a.shape[2], width), dtype),
        scratch_shapes=[
            pltpu.VMEM((NX, NY, 2, a.shape[1] // 2, width), a.dtype),
            pltpu.SemaphoreType.DMA((8,)),
        ],
        compiler_params=pltpu.CompilerParams(vmem_limit_bytes=VMEM),
    )(spot, a, *pieces)


def adam_update(weights, first, second, gradient):
    first = BETA_ONE * first + (1.0 - BETA_ONE) * gradient
    second = BETA_TWO * second + (1.0 - BETA_TWO) * gradient * gradient
    weights = weights - INNER_RATE * (first / (jnp.sqrt(second) + EPSILON) + DECAY * weights)
    return weights, first, second


def adam_kernel(
    spot, anchor, first, second, own_a, got_a, own_b, got_b, scale, decoded, new_first, new_second
):
    start = anchor[...]
    weights, one, two = start, first[0], second[0]
    for own, got in ((own_a, got_a), (own_b, got_b)):
        gradient = own[...] + got[...].astype(jnp.float32)
        weights, one, two = adam_update(weights, one, two, gradient)
    new_first[0] = one
    new_second[0] = two
    delta = start - weights
    factors = jnp.left_shift(jnp.ones_like(scale[0]), -scale[0]).astype(jnp.float32)
    for block in range(delta.shape[1] // 128):
        columns = slice(block * 128, (block + 1) * 128)
        factor = factors[:, block : block + 1]
        coded = jnp.clip(delta[:, columns] * factor, -CODE_LIMIT, CODE_LIMIT).astype(jnp.bfloat16)
        decoded[:, columns] = (coded.astype(jnp.float32) / factor).astype(jnp.bfloat16)


def adam(spot, anchor, first, second, own_a, got_a, own_b, got_b, exponents):
    rows, width = anchor.shape
    tile = 32
    steps = rows // tile
    flat = pl.BlockSpec((tile, width), lambda i, spot: (i, 0))
    deep = pl.BlockSpec((1, tile, width), lambda i, spot: (0, i, 0))
    return pl.pallas_call(
        adam_kernel,
        grid_spec=pltpu.PrefetchScalarGridSpec(
            num_scalar_prefetch=1,
            grid=(steps,),
            in_specs=[flat, deep, deep, flat, flat, flat, flat]
            + [pl.BlockSpec((1, tile, exponents.shape[2]), lambda i, spot: (0, i, 0))],
            out_specs=[flat, deep, deep],
        ),
        out_shape=[
            jax.ShapeDtypeStruct((rows, width), jnp.bfloat16),
            jax.ShapeDtypeStruct(first.shape, jnp.float32),
            jax.ShapeDtypeStruct(second.shape, jnp.float32),
        ],
    )(spot, anchor, first, second, own_a, got_a, own_b, got_b, exponents)


def replica_sum(decoded):
    rows, width = decoded.shape
    place = lax.axis_index("replica")
    line, core = place // CORES, place % CORES
    halves = decoded.reshape(CORES, rows // CORES, width)
    keep = lax.dynamic_index_in_dim(halves, core, 0, keepdims=False)
    send = lax.dynamic_index_in_dim(halves, 1 - core, 0, keepdims=False)
    got = lax.ppermute(send, "replica", replica_shift(0, 1))
    half = (keep.astype(jnp.float32) + got.astype(jnp.float32)).astype(jnp.bfloat16)
    parts = half.reshape(LINE, -1, width)
    total = lax.dynamic_index_in_dim(parts, line, 0, keepdims=False).astype(jnp.float32)
    for turn in (1, 2, 3):
        part = lax.dynamic_index_in_dim(parts, lax.rem(line + turn, LINE), 0, keepdims=False)
        got = lax.ppermute(part, "replica", replica_shift(turn, 0))
        total = total + got.astype(jnp.float32)
    total = total.astype(jnp.bfloat16)
    whole = [total]
    for turn in (1, 2, 3):
        whole.append(lax.ppermute(total, "replica", replica_shift(turn, 0)))
    order = lax.rem(line - jnp.arange(LINE, dtype=jnp.int32) + LINE, LINE)
    half = jnp.take(jnp.stack(whole), order, axis=0).reshape(-1, width)
    other = lax.ppermute(half, "replica", replica_shift(0, 1))
    even = core == 0
    return jnp.concatenate([jnp.where(even, half, other), jnp.where(even, other, half)])


def on_device(
    anchor, first_moment, second_moment, outer_momentum, activations, cotangents, token_ids, exponents
):
    place = lax.axis_index("fsdp").astype(jnp.int32)
    z, x, y = place // PLANE, (place // NY) % NX, place % NY
    masked = jnp.where((token_ids[0] != 0)[..., None], cotangents[0], jnp.zeros_like(cotangents[0]))
    half = masked.shape[1] // 2

    sent = {}
    for step in range(2):
        for mine in (0, 1):
            side = jnp.where(mine == 1, z, 1 - z)
            sent[step, mine] = split_rows(side.reshape(1), activations, step)

    early = ring_gather(masked[:, :half], X_RING)
    late = ring_gather(masked[:, half:], Y_RING)
    early = ring_gather(stack_pieces(early, x), Y_RING)
    late = ring_gather(stack_pieces(late, y), X_RING)
    sets = (early, late)

    spot = jnp.stack([x, y])
    got, own = {}, {}
    columns = {}
    for mine, step in ((0, 0), (0, 1), (1, 0), (1, 1)):
        columns[step, mine] = lax.all_to_all(
            sent[step, mine], "fsdp", 0, 0, axis_index_groups=PLANES, tiled=True
        )
    for step in range(2):
        part = contract(spot, columns[step, 0], sets, step, jnp.bfloat16)
        got[step] = lax.ppermute(part, "fsdp", Z_SWAP)
    for step in range(2):
        own[step] = contract(spot, columns[step, 1], sets, step, jnp.float32)

    decoded, new_first, new_second = adam(
        spot, anchor, first_moment, second_moment, own[0], got[0], own[1], got[1], exponents
    )
    replicas = lax.axis_size("replica")
    average = replica_sum(decoded).astype(jnp.float32) / replicas
    new_momentum = MOMENTUM * outer_momentum + average
    new_weights = anchor - OUTER_RATE * (average + MOMENTUM * new_momentum)
    return new_weights, new_momentum, new_first, new_second


def solution(mesh):
    in_specs = (
        P("fsdp", None),
        P("replica", "fsdp", None),
        P("replica", "fsdp", None),
        P("fsdp", None),
        P("replica", None, "fsdp", None),
        P("replica", None, "fsdp", None),
        P("replica", None, "fsdp"),
        P("replica", "fsdp", None),
    )
    out_specs = (
        P("fsdp", None),
        P("fsdp", None),
        P("replica", "fsdp", None),
        P("replica", "fsdp", None),
    )
    return jax.shard_map(
        on_device, mesh=mesh, in_specs=in_specs, out_specs=out_specs, check_vma=False
    )
```

```python
import functools

import jax
import jax.numpy as jnp
from jax import lax
from jax.experimental import pallas as pl
from jax.experimental.pallas import tpu as pltpu
from jax.sharding import PartitionSpec as P

BETA_ONE = 0.9
BETA_TWO = 0.95
EPSILON = 1e-08
INNER_RATE = 0.1
DECAY = 0.1
OUTER_RATE = 0.7
MOMENTUM = 0.9
CODE_LIMIT = 448.0
LOWEST = 13

NZ, NX, NY = 2, 4, 4
PLANE = NX * NY
LINE, CORES = 4, 2
LIMIT = 12 * 1024 * 1024

HBM = pl.BlockSpec(memory_space=pltpu.HBM)
VMEM = pl.BlockSpec(memory_space=pltpu.VMEM)
SMEM = pl.BlockSpec(memory_space=pltpu.SMEM)
PARAMS = pltpu.CompilerParams(vmem_limit_bytes=LIMIT)
SHORT = pl.CostEstimate(flops=1, bytes_accessed=1, transcendentals=0)


def fsdp_shift(dz, dx, dy):
    def at(z, x, y):
        return ((z % NZ) * NX + x % NX) * NY + y % NY

    return [
        (at(z, x, y), at(z + dz, x + dx, y + dy))
        for z in range(NZ)
        for x in range(NX)
        for y in range(NY)
    ]


def replica_shift(dz, dc):
    return [
        (z * CORES + c, ((z + dz) % LINE) * CORES + (c + dc) % CORES)
        for z in range(LINE)
        for c in range(CORES)
    ]


def along(dim, block, turn):
    shift = (0, turn, 0) if dim == "x" else (0, 0, turn)
    return lax.ppermute(block, "fsdp", fsdp_shift(*shift))


def after(value, earlier):
    return lax.optimization_barrier((value, earlier))[0]


def shape_of(shape, dtype):
    return jax.ShapeDtypeStruct(shape, dtype)


HANDED = 10


def pack_kernel(dim, step, spot, ids, cotangents, features, own, ahead, back, *scratch):
    held, words, grads, sems = scratch
    tokens, shard = own.shape[1:]
    part = tokens // 4
    small = [
        pltpu.make_async_copy(ids, words, sems.at[4]),
        pltpu.make_async_copy(cotangents.at[0, step], grads, sems.at[5]),
    ]
    loads = []
    for q in range(4):
        rows = pl.ds(q * part, part)
        loads.append(pltpu.make_async_copy(features.at[0, step, rows], held.at[rows], sems.at[q]))
    for load in small + loads:
        load.start()
    for load in small:
        load.wait()
    live = jnp.sum((words[0, step : step + 1, :] != 0).astype(jnp.int32))
    alive = lax.broadcasted_iota(jnp.int32, (tokens, shard), 0) < live
    for n in range(4):
        block = grads[:, n * shard : (n + 1) * shard]
        block = jnp.where(alive, block, jnp.zeros_like(block))
        own[8 + n] = block
        ahead[8 + (n + 2) % 4] = block
        back[8 + n] = block
    x, y, z = spot[0], spot[1], spot[4]
    for q, load in enumerate(loads):
        load.wait()
        rows = slice(q * part, (q + 1) * part)
        for turn in range(4):
            for side in range(2):
                for u in range(4):
                    to_x, to_y = (u, turn) if dim == "y" else (turn, u)
                    owner = (lax.rem(z + 1 + side, NZ) * NX + lax.rem(x + to_x, NX)) * NY
                    owner = owner + lax.rem(y + to_y, NY)
                    at = pl.ds(pl.multiple_of(owner * shard, shard), shard)
                    out, slot = (own, ahead, back if side else ahead, back)[turn], side * 4 + u
                    out[12 + u if turn == 2 else slot, rows, :] = held[rows, at]


def pack(dim, step, spot, ids, cotangents, features):
    tokens, rows = features.shape[2:]
    shard = rows // (NZ * NX * NY)
    return pl.pallas_call(
        functools.partial(pack_kernel, dim, step),
        in_specs=[SMEM, HBM, HBM, HBM],
        out_specs=[VMEM] * 3,
        out_shape=[shape_of((blocks, tokens, shard), features.dtype) for blocks in (12, 16, 16)],
        scratch_shapes=[
            pltpu.VMEM((tokens, rows), features.dtype),
            pltpu.VMEM(ids.shape, ids.dtype),
            pltpu.VMEM(cotangents.shape[2:], cotangents.dtype),
            pltpu.SemaphoreType.DMA((6,)),
        ],
        cost_estimate=SHORT,
        compiler_params=PARAMS,
    )(spot, ids, cotangents, features)


def products(side, turn, pieces):
    own, ahead, back, handed_ahead, handed_back = pieces
    slot = side * 4 + turn
    handed = handed_back if side else handed_ahead
    left = jnp.concatenate([own[slot], ahead[slot], back[slot], handed[2 + turn]], axis=0)
    for n in range(4):
        far = (handed_back if n // 2 else handed_ahead)[n % 2]
        right = jnp.concatenate([own[8 + n], ahead[8 + (n + 2) % 4], back[8 + n], far], axis=0)
        yield n, lax.dot_general(
            left, right, (((0,), (0,)), ((), ())), preferred_element_type=jnp.float32
        )


def opposite_kernel(side, *refs):
    for step in range(2):
        pieces, (low, high) = refs[5 * step : 5 * step + 5], refs[10 + 2 * step : 12 + 2 * step]
        shard, half = pieces[0].shape[2], low.shape[0]
        for n, value in products(side, 2, pieces):
            low[:, n * shard : (n + 1) * shard] = value[:half].astype(low.dtype)
            high[:, n * shard : (n + 1) * shard] = value[half:].astype(high.dtype)


def opposite(side, pieces):
    _, _, shard = pieces[0].shape
    out = shape_of((shard // 2, 4 * shard), pieces[0].dtype)
    return pl.pallas_call(
        functools.partial(opposite_kernel, side),
        in_specs=[VMEM] * 10, out_specs=[VMEM] * 4, out_shape=[out] * 4,
        cost_estimate=SHORT, compiler_params=PARAMS,
    )(*pieces)


def nearest_kernel(side, *refs):
    for step in range(2):
        pieces, (low, high) = refs[5 * step : 5 * step + 5], refs[10 + 2 * step : 12 + 2 * step]
        own, ahead, back = refs[14 + 3 * step : 17 + 3 * step]
        shard, half = pieces[0].shape[2], low.shape[0]
        for n, value in products(side, 1, pieces):
            at = slice(n * shard, (n + 1) * shard)
            ahead[:half, at] = (value[:half] + low[:, at].astype(jnp.float32)).astype(ahead.dtype)
            ahead[half:, at] = value[half:].astype(ahead.dtype)
        for n, value in products(side, 3, pieces):
            at = slice(n * shard, (n + 1) * shard)
            back[:half, at] = value[:half].astype(back.dtype)
            back[half:, at] = (value[half:] + high[:, at].astype(jnp.float32)).astype(back.dtype)
        for n, value in products(side, 0, pieces):
            own[:, n * shard : (n + 1) * shard] = value


def nearest(side, pieces, halves):
    _, _, shard = pieces[0].shape
    shape = (shard, 4 * shard)
    sent = shape_of(shape, pieces[0].dtype)
    out = [shape_of(shape, jnp.float32), sent, sent]
    return pl.pallas_call(
        functools.partial(nearest_kernel, side),
        in_specs=[VMEM] * 14, out_specs=[VMEM] * 6, out_shape=out * 2,
        cost_estimate=SHORT, compiler_params=PARAMS,
    )(*pieces, *halves)


def total_kernel(*refs):
    ins, out = refs[:-1], refs[-1]

    @pl.loop(0, out.shape[1], step=16)
    def _(r):
        rows = pl.ds(pl.multiple_of(r, 16), 16)
        for step in range(2):
            total = ins[3 * step][rows, :]
            for ref in ins[3 * step + 1 : 3 * step + 3]:
                total = total + ref[rows, :].astype(jnp.float32)
            out[step, rows, :] = total.astype(out.dtype)


def totals(parts, dtype):
    return pl.pallas_call(
        total_kernel, in_specs=[VMEM] * 6, out_specs=VMEM,
        out_shape=shape_of((2,) + parts[0].shape, dtype), cost_estimate=SHORT, compiler_params=PARAMS,
    )(*parts)


def add_kernel(*refs):
    ins, out = refs[:-1], refs[-1]

    @pl.loop(0, out.shape[0], step=16)
    def _(r):
        rows = pl.ds(pl.multiple_of(r, 16), 16)
        total = ins[0][rows, :].astype(jnp.float32)
        for ref in ins[1:]:
            total = total + ref[rows, :].astype(jnp.float32)
        out[rows, :] = total.astype(out.dtype)


def add(parts, dtype):
    return pl.pallas_call(
        add_kernel, in_specs=[VMEM] * len(parts), out_specs=VMEM,
        out_shape=shape_of(parts[0].shape, dtype), cost_estimate=SHORT, compiler_params=PARAMS,
    )(*parts)


def adam_update(weights, first, second, gradient):
    first = BETA_ONE * first + (1.0 - BETA_ONE) * gradient
    second = BETA_TWO * second + (1.0 - BETA_TWO) * gradient * gradient
    weights = weights - INNER_RATE * (first / (jnp.sqrt(second) + EPSILON) + DECAY * weights)
    return weights, first, second


def gradient_of(step, own, got, here):
    here = (step,) + here
    return own[here] + got[here].astype(jnp.float32)


def early_kernel(anchor, first, second, own, got, mid_weights, mid_first, mid_second):
    @pl.loop(0, anchor.shape[0], step=16)
    def _(r):
        rows = pl.ds(pl.multiple_of(r, 16), 16)
        for c in range(0, anchor.shape[1], 256):
            here = (rows, pl.ds(c, 256))
            mid_weights[here], mid_first[here], mid_second[here] = adam_update(
                anchor[here], first[(0,) + here], second[(0,) + here], gradient_of(0, own, got, here)
            )


def early_step(anchor, first, second, own, got):
    out = shape_of(anchor.shape, jnp.float32)
    return pl.pallas_call(
        early_kernel, in_specs=[VMEM] * 5, out_specs=[VMEM] * 3, out_shape=[out] * 3,
        cost_estimate=SHORT, compiler_params=PARAMS,
    )(anchor, first, second, own, got)


def code_kernel(spot, anchor, weights, first, second, own, got, scale, send, keep):
    half = anchor.shape[0] // CORES
    for side, out in ((1, send), (0, keep)):
        base = lax.rem(spot[2] + side, CORES) * half

        @pl.loop(0, half, step=16)
        def _(r, base=base, out=out):
            rows = pl.ds(pl.multiple_of(base + r, 16), 16)
            for c in range(0, anchor.shape[1], 256):
                here = (rows, pl.ds(c, 256))
                gradient = gradient_of(1, own, got, here)
                end = adam_update(weights[here], first[here], second[here], gradient)[0]
                delta = anchor[here] - end
                for block in range(2):
                    at = c // 128 + block
                    power = jnp.broadcast_to(scale[0, rows, at : at + 1], (16, 128))
                    ones = jnp.ones_like(power)
                    factor = jnp.left_shift(ones, -power).astype(jnp.float32)
                    back = jnp.left_shift(ones, power + LOWEST).astype(jnp.float32) * 2.0**-LOWEST
                    coded = delta[:, block * 128 : (block + 1) * 128] * factor
                    coded = jnp.clip(coded, -CODE_LIMIT, CODE_LIMIT).astype(jnp.bfloat16)
                    out[pl.ds(pl.multiple_of(r, 16), 16), pl.ds(at * 128, 128)] = (
                        coded.astype(jnp.float32) * back
                    ).astype(jnp.bfloat16)


def code(spot, anchor, weights, first, second, own, got, exponents):
    rows, width = anchor.shape
    part = shape_of((rows // CORES, width), jnp.bfloat16)
    return pl.pallas_call(
        code_kernel, in_specs=[SMEM] + [VMEM] * 7, out_specs=[VMEM] * 2, out_shape=[part] * 2,
        cost_estimate=SHORT, compiler_params=PARAMS,
    )(spot, anchor, weights, first, second, own, got, exponents)


def moment_kernel(first, second, own, got, new_first, new_second):
    @pl.loop(0, first.shape[0], step=16)
    def _(r):
        rows = pl.ds(pl.multiple_of(r, 16), 16)
        for c in range(0, first.shape[1], 256):
            here = (rows, pl.ds(c, 256))
            gradient = gradient_of(1, own, got, here)
            _, one, two = adam_update(first[here], first[here], second[here], gradient)
            new_first[(0,) + here] = one
            new_second[(0,) + here] = two


def moments(first, second, own, got):
    out = shape_of((1,) + first.shape, first.dtype)
    return pl.pallas_call(
        moment_kernel, in_specs=[VMEM] * 4, out_specs=[VMEM] * 2, out_shape=[out] * 2,
        cost_estimate=SHORT, compiler_params=PARAMS,
    )(first, second, own, got)


def pair_kernel(spot, keep, got, *outs):
    rows = outs[0].shape[0]
    for turn, out in enumerate(outs):
        at = pl.ds(pl.multiple_of(lax.rem(spot[3] + turn, LINE) * rows, rows), rows)
        total = keep[at, :].astype(jnp.float32) + got[at, :].astype(jnp.float32)
        out[...] = total.astype(out.dtype)


def pair_sum(spot, keep, got):
    rows, width = keep.shape
    out = shape_of((rows // LINE, width), keep.dtype)
    return pl.pallas_call(
        pair_kernel, in_specs=[SMEM, VMEM, VMEM], out_specs=[VMEM] * LINE, out_shape=[out] * LINE,
        cost_estimate=SHORT, compiler_params=PARAMS,
    )(spot, keep, got)


def join_kernel(spot, *refs):
    out = refs[-1]
    rows = refs[0].shape[0]
    for turn, ref in enumerate(refs[:-1]):
        at = pl.ds(pl.multiple_of(lax.rem(spot[3] - turn + LINE, LINE) * rows, rows), rows)
        out[at, :] = ref[...]


def join(spot, parts):
    rows, width = parts[0].shape
    return pl.pallas_call(
        join_kernel, in_specs=[SMEM] + [VMEM] * len(parts), out_specs=VMEM,
        out_shape=shape_of((rows * len(parts), width), parts[0].dtype), cost_estimate=SHORT, compiler_params=PARAMS,
    )(spot, *parts)


def replica_sum(spot, got, keep, late):
    parts = pair_sum(spot, keep, got)
    total = [parts[0]]
    for turn in (1, 2, 3):
        total.append(lax.ppermute(parts[turn], "replica", replica_shift(turn, 0)))
    total = add(total, jnp.bfloat16)
    whole = [total]
    for turn in (1, 2, 3):
        whole.append(lax.ppermute(total, "replica", replica_shift(turn, 0)))
    half = join(after(spot, late), whole)
    other = lax.ppermute(half, "replica", replica_shift(0, 1))
    even = spot[2] == 0
    return jnp.concatenate([jnp.where(even, half, other), jnp.where(even, other, half)])


def on_device(
    anchor, first_moment, second_moment, outer_momentum, activations, cotangents, token_ids, exponents
):
    place = lax.axis_index("fsdp").astype(jnp.int32)
    z, x, y = place // PLANE, (place // NY) % NX, place % NY
    copy = lax.axis_index("replica").astype(jnp.int32)
    spot = jnp.stack([x, y, copy % CORES, copy // CORES, z])

    rings = ("y", "x")

    sent = [pack("y", 0, spot, token_ids, cotangents, activations)]
    sent.append(pack("x", 1, spot, token_ids, cotangents, activations))
    ahead = [along(ring, block[1], 1) for ring, block in zip(rings, sent)]
    back = [along(ring, block[2], -1) for ring, block in zip(rings, sent)]
    handed_ahead = [along(ring, block[HANDED:], 1) for ring, block in zip(rings, ahead)]
    handed_back = [along(ring, block[HANDED:], -1) for ring, block in zip(rings, back)]
    pieces = []
    for step in range(2):
        pieces += [sent[step][0], ahead[step], back[step], handed_ahead[step], handed_back[step]]

    def reduce(side, pieces, dtype):
        low_a, high_a, low_b, high_b = opposite(side, pieces)
        halves = along("x", low_a, 1), along("x", high_a, -1), along("y", low_b, 1), along("y", high_b, -1)
        own_a, ahead_a, back_a, own_b, ahead_b, back_b = nearest(side, pieces, halves)
        parts = own_a, along("x", ahead_a, 1), along("x", back_a, -1)
        parts += own_b, along("y", ahead_b, 1), along("y", back_b, -1)
        return totals(parts, dtype)

    theirs = reduce(0, pieces, jnp.bfloat16)
    got = lax.ppermute(theirs, "fsdp", fsdp_shift(1, 0, 0))
    own = reduce(1, lax.optimization_barrier(pieces + [theirs])[:-1], jnp.float32)

    weights, first, second = early_step(anchor, first_moment, second_moment, own, got)
    send, keep = code(spot, anchor, weights, first, second, own, got, exponents)
    other = lax.ppermute(send, "replica", replica_shift(0, 1))
    new_first, new_second = moments(first, second, own, after(got, other))
    replicas = lax.axis_size("replica")
    average = replica_sum(spot, other, keep, new_first).astype(jnp.float32) / replicas
    new_momentum = MOMENTUM * outer_momentum + average
    new_weights = anchor - OUTER_RATE * (average + MOMENTUM * new_momentum)
    return new_weights, new_momentum, new_first, new_second


def solution(mesh):
    in_specs = (
        P("fsdp", None),
        P("replica", "fsdp", None),
        P("replica", "fsdp", None),
        P("fsdp", None),
        P("replica", None, "fsdp", None),
        P("replica", None, "fsdp", None),
        P("replica", None, "fsdp"),
        P("replica", "fsdp", None),
    )
    out_specs = (
        P("fsdp", None),
        P("fsdp", None),
        P("replica", "fsdp", None),
        P("replica", "fsdp", None),
    )
    return jax.shard_map(
        on_device, mesh=mesh, in_specs=in_specs, out_specs=out_specs, check_vma=False
    )
```

```python
import functools

import jax
import jax.numpy as jnp
from jax import lax
from jax.experimental import pallas as pl
from jax.experimental.pallas import tpu as pltpu
from jax.sharding import PartitionSpec as P

BETA_ONE = 0.9
BETA_TWO = 0.95
EPSILON = 1e-08
INNER_RATE = 0.1
DECAY = 0.1
OUTER_RATE = 0.7
MOMENTUM = 0.9
CODE_LIMIT = 448.0
LOWEST = 13

NZ, NX, NY = 2, 4, 4
PLANE = NX * NY
LINE, CORES = 4, 2
LIMIT = 12 * 1024 * 1024

HBM = pl.BlockSpec(memory_space=pltpu.HBM)
VMEM = pl.BlockSpec(memory_space=pltpu.VMEM)
SMEM = pl.BlockSpec(memory_space=pltpu.SMEM)
PARAMS = pltpu.CompilerParams(vmem_limit_bytes=LIMIT)
SHORT = pl.CostEstimate(flops=1, bytes_accessed=1, transcendentals=0)


def fsdp_shift(dz, dx, dy):
    def at(z, x, y):
        return ((z % NZ) * NX + x % NX) * NY + y % NY

    return [
        (at(z, x, y), at(z + dz, x + dx, y + dy))
        for z in range(NZ)
        for x in range(NX)
        for y in range(NY)
    ]


def along(dim, block, turn):
    shift = (0, turn, 0) if dim == "x" else (0, 0, turn)
    return lax.ppermute(block, "fsdp", fsdp_shift(*shift))


def after(value, earlier):
    return lax.optimization_barrier((value, earlier))[0]


def shape_of(shape, dtype):
    return jax.ShapeDtypeStruct(shape, dtype)


def pack_kernel(dim, step, spot, ids, cotangents, features, own, ahead, back, ahead_late, back_late, *scratch):
    held, words, grads, sems = scratch
    tokens, shard = own.shape[1:]
    part = tokens // 4
    small = [
        pltpu.make_async_copy(ids, words, sems.at[4]),
        pltpu.make_async_copy(cotangents.at[0, step], grads, sems.at[5]),
    ]
    loads = []
    for q in range(4):
        rows = pl.ds(q * part, part)
        loads.append(pltpu.make_async_copy(features.at[0, step, rows], held.at[rows], sems.at[q]))
    for load in small + loads:
        load.start()
    for load in small:
        load.wait()
    live = jnp.sum((words[0, step : step + 1, :] != 0).astype(jnp.int32))
    alive = lax.broadcasted_iota(jnp.int32, (tokens, shard), 0) < live
    for n in range(4):
        block = grads[:, n * shard : (n + 1) * shard]
        block = jnp.where(alive, block, jnp.zeros_like(block))
        own[8 + n] = block
        ahead[4 + (n + 2) % 4] = block
        back[4 + n] = block
    x, y, z = spot[0], spot[1], spot[4]
    places = {}
    for u in range(4):
        for side, (to_ahead, to_back) in enumerate(((ahead, back), (ahead_late, back_late))):
            far = (to_ahead, to_back)[u // 2]
            places[side, 0, u] = own, 4 * side + u
            places[side, 1, u] = to_ahead, u
            places[side, 2, u] = far, far.shape[0] - 2 + u % 2
            places[side, 3, u] = to_back, u
    for q, load in enumerate(loads):
        load.wait()
        rows = slice(q * part, (q + 1) * part)
        for (side, turn, u), (out, slot) in places.items():
            to_x, to_y = (u, turn) if dim == "y" else (turn, u)
            owner = (lax.rem(z + 1 + side, NZ) * NX + lax.rem(x + to_x, NX)) * NY
            owner = owner + lax.rem(y + to_y, NY)
            at = pl.ds(pl.multiple_of(owner * shard, shard), shard)
            out[slot, rows, :] = held[rows, at]


def pack(dim, step, spot, ids, cotangents, features):
    tokens, rows = features.shape[2:]
    shard = rows // (NZ * NX * NY)
    return pl.pallas_call(
        functools.partial(pack_kernel, dim, step),
        in_specs=[SMEM, HBM, HBM, HBM],
        out_specs=[VMEM] * 5,
        out_shape=[shape_of((blocks, tokens, shard), features.dtype) for blocks in (12, 10, 10, 6, 6)],
        scratch_shapes=[
            pltpu.VMEM((tokens, rows), features.dtype),
            pltpu.VMEM(ids.shape, ids.dtype),
            pltpu.VMEM(cotangents.shape[2:], cotangents.dtype),
            pltpu.SemaphoreType.DMA((6,)),
        ],
        cost_estimate=SHORT,
        compiler_params=PARAMS,
    )(spot, ids, cotangents, features)


def products(turn, pieces):
    own, ahead, back = pieces[:3]
    handed = pieces[3:5]
    if len(pieces) == 5:
        left = [own[turn], ahead[turn], back[turn], handed[turn // 2][2 + turn % 2]]
    else:
        late = pieces[5:]
        left = [own[4 + turn], late[0][turn], late[1][turn], late[2 + turn // 2][turn % 2]]
    left = jnp.concatenate(left, axis=0)
    for n in range(4):
        right = [own[8 + n], ahead[4 + (n + 2) % 4], back[4 + n], handed[n // 2][n % 2]]
        yield n, lax.dot_general(
            left,
            jnp.concatenate(right, axis=0),
            (((0,), (0,)), ((), ())),
            preferred_element_type=jnp.float32,
        )


def opposite_kernel(*refs):
    pieces, (low, high) = refs[:-2], refs[-2:]
    shard, half = pieces[0].shape[2], low.shape[0]
    for n, value in products(2, pieces):
        low[:, n * shard : (n + 1) * shard] = value[:half].astype(low.dtype)
        high[:, n * shard : (n + 1) * shard] = value[half:].astype(high.dtype)


def opposite(pieces):
    _, _, shard = pieces[0].shape
    out = shape_of((shard // 2, 4 * shard), pieces[0].dtype)
    return pl.pallas_call(
        opposite_kernel, in_specs=[VMEM] * len(pieces), out_specs=[VMEM] * 2, out_shape=[out] * 2,
        cost_estimate=SHORT, compiler_params=PARAMS,
    )(*pieces)


def nearest_kernel(*refs):
    pieces, (low, high, own, ahead, back) = refs[:-5], refs[-5:]
    shard, half = pieces[0].shape[2], low.shape[0]
    for n, value in products(1, pieces):
        at = slice(n * shard, (n + 1) * shard)
        ahead[:half, at] = (value[:half] + low[:, at].astype(jnp.float32)).astype(ahead.dtype)
        ahead[half:, at] = value[half:].astype(ahead.dtype)
    for n, value in products(3, pieces):
        at = slice(n * shard, (n + 1) * shard)
        back[:half, at] = value[:half].astype(back.dtype)
        back[half:, at] = (value[half:] + high[:, at].astype(jnp.float32)).astype(back.dtype)
    for n, value in products(0, pieces):
        own[:, n * shard : (n + 1) * shard] = value


def nearest(pieces, low, high):
    _, _, shard = pieces[0].shape
    shape = (shard, 4 * shard)
    sent = shape_of(shape, pieces[0].dtype)
    return pl.pallas_call(
        nearest_kernel, in_specs=[VMEM] * (len(pieces) + 2), out_specs=[VMEM] * 3,
        out_shape=[shape_of(shape, jnp.float32), sent, sent],
        cost_estimate=SHORT, compiler_params=PARAMS,
    )(*pieces, low, high)


def total_kernel(*refs):
    ins, out = refs[:-1], refs[-1]

    @pl.loop(0, out.shape[1], step=16)
    def _(r):
        rows = pl.ds(pl.multiple_of(r, 16), 16)
        for step in range(2):
            total = ins[3 * step][rows, :]
            for ref in ins[3 * step + 1 : 3 * step + 3]:
                total = total + ref[rows, :].astype(jnp.float32)
            out[step, rows, :] = total.astype(out.dtype)


def totals(parts, dtype):
    return pl.pallas_call(
        total_kernel, in_specs=[VMEM] * 6, out_specs=VMEM,
        out_shape=shape_of((2,) + parts[0].shape, dtype), cost_estimate=SHORT, compiler_params=PARAMS,
    )(*parts)


def add_kernel(*refs):
    total = refs[0][...].astype(jnp.float32)
    for ref in refs[1:-1]:
        total = total + ref[...].astype(jnp.float32)
    refs[-1][...] = total.astype(refs[-1].dtype)


def add(parts):
    return pl.pallas_call(
        add_kernel, in_specs=[VMEM] * len(parts), out_specs=VMEM,
        out_shape=shape_of(parts[0].shape, parts[0].dtype), cost_estimate=SHORT, compiler_params=PARAMS,
    )(*parts)


def adam_update(weights, first, second, gradient):
    first = BETA_ONE * first + (1.0 - BETA_ONE) * gradient
    second = BETA_TWO * second + (1.0 - BETA_TWO) * gradient * gradient
    weights = weights - INNER_RATE * (first / (jnp.sqrt(second) + EPSILON) + DECAY * weights)
    return weights, first, second


def inner_steps(anchor, first, second, own, got, here):
    weights, one, two = anchor[here], first[(0,) + here], second[(0,) + here]
    for step in range(own.shape[0]):
        at = (step,) + here
        gradient = own[at] + got[at].astype(jnp.float32)
        weights, one, two = adam_update(weights, one, two, gradient)
    return weights, one, two


def code_kernel(turn, spot, anchor, first, second, own, got, scale, out):
    half = out.shape[0]
    base = lax.rem(spot[2] + turn, CORES) * half

    @pl.loop(0, half, step=16)
    def _(r):
        rows = pl.ds(pl.multiple_of(base + r, 16), 16)
        for c in range(0, anchor.shape[1], 256):
            here = (rows, pl.ds(c, 256))
            delta = anchor[here] - inner_steps(anchor, first, second, own, got, here)[0]
            for block in range(2):
                at = c // 128 + block
                power = jnp.broadcast_to(scale[0, rows, at : at + 1], (16, 128))
                ones = jnp.ones_like(power)
                factor = jnp.left_shift(ones, -power).astype(jnp.float32)
                back = jnp.left_shift(ones, power + LOWEST).astype(jnp.float32) * 2.0**-LOWEST
                coded = delta[:, block * 128 : (block + 1) * 128] * factor
                coded = jnp.clip(coded, -CODE_LIMIT, CODE_LIMIT).astype(jnp.bfloat16)
                out[pl.ds(pl.multiple_of(r, 16), 16), pl.ds(at * 128, 128)] = (
                    coded.astype(jnp.float32) * back
                ).astype(jnp.bfloat16)


def code(turn, spot, anchor, first, second, own, got, exponents):
    rows, width = anchor.shape
    return pl.pallas_call(
        functools.partial(code_kernel, turn),
        in_specs=[SMEM] + [VMEM] * 6, out_specs=VMEM,
        out_shape=shape_of((rows // CORES, width), jnp.bfloat16),
        cost_estimate=SHORT, compiler_params=PARAMS,
    )(spot, anchor, first, second, own, got, exponents)


def moment_kernel(anchor, first, second, own, got, new_first, new_second):
    @pl.loop(0, anchor.shape[0], step=16)
    def _(r):
        rows = pl.ds(pl.multiple_of(r, 16), 16)
        for c in range(0, anchor.shape[1], 256):
            here = (rows, pl.ds(c, 256))
            _, one, two = inner_steps(anchor, first, second, own, got, here)
            new_first[(0,) + here] = one
            new_second[(0,) + here] = two


def moments(anchor, first, second, own, got):
    out = shape_of(first.shape, first.dtype)
    return pl.pallas_call(
        moment_kernel, in_specs=[VMEM] * 5, out_specs=[VMEM] * 2, out_shape=[out] * 2,
        cost_estimate=SHORT, compiler_params=PARAMS,
    )(anchor, first, second, own, got)


def pair_kernel(spot, ours, got, keep, send):
    rows = keep.shape[0]
    for turn, out in ((1, send), (0, keep)):
        at = pl.ds(pl.multiple_of(lax.rem(spot[3] + turn, 2) * rows, rows), rows)
        total = ours[at, :].astype(jnp.float32) + got[at, :].astype(jnp.float32)
        out[...] = total.astype(out.dtype)


def pair_sum(spot, ours, got):
    rows, width = ours.shape
    out = shape_of((rows // 2, width), ours.dtype)
    return pl.pallas_call(
        pair_kernel, in_specs=[SMEM, VMEM, VMEM], out_specs=[VMEM] * 2, out_shape=[out] * 2,
        cost_estimate=SHORT, compiler_params=PARAMS,
    )(spot, ours, got)


def join_kernel(spot, ours, got, out):
    rows = ours.shape[0]
    for turn, ref in ((0, ours), (1, got)):
        at = pl.ds(pl.multiple_of(lax.rem(spot[3] + turn, 2) * rows, rows), rows)
        out[at, :] = ref[...]


def join(spot, ours, got):
    rows, width = ours.shape
    return pl.pallas_call(
        join_kernel, in_specs=[SMEM, VMEM, VMEM], out_specs=VMEM,
        out_shape=shape_of((2 * rows, width), ours.dtype), cost_estimate=SHORT, compiler_params=PARAMS,
    )(spot, ours, got)


def swap(block, line, core):
    pairs = [
        (z * CORES + c, (z ^ line) * CORES + (c ^ core)) for z in range(LINE) for c in range(CORES)
    ]
    return lax.ppermute(block, "replica", pairs)


def outer_kernel(turn, spot, total, anchor, momentum, *refs):
    new_weights, new_momentum, weights, moving, sems = refs[-5:]
    rows = total.shape[0]
    base = lax.rem(spot[2] + turn, CORES) * rows
    tile = rows // 4
    stores = []
    for r in range(0, rows, tile):
        here = pl.ds(pl.multiple_of(base + r, tile), tile)
        average = total[r : r + tile, :].astype(jnp.float32) * (1.0 / (LINE * CORES))
        moved = MOMENTUM * momentum[here, :] + average
        moving[r : r + tile, :] = moved
        weights[r : r + tile, :] = anchor[here, :] - OUTER_RATE * (average + MOMENTUM * moved)
        for k, (held, out) in enumerate(((moving, new_momentum), (weights, new_weights))):
            store = pltpu.make_async_copy(
                held.at[pl.ds(r, tile)], out.at[here], sems.at[k, r // tile]
            )
            store.start()
            stores.append(store)
    for store in stores:
        store.wait()


def outer_step(turn, spot, total, anchor, momentum, outs=()):
    rows, width = total.shape
    return pl.pallas_call(
        functools.partial(outer_kernel, turn),
        in_specs=[SMEM] + [VMEM] * 3 + [HBM] * len(outs),
        out_specs=[HBM] * 2,
        out_shape=[shape_of(anchor.shape, anchor.dtype)] * 2,
        scratch_shapes=[
            pltpu.VMEM((rows, width), jnp.float32),
            pltpu.VMEM((rows, width), jnp.float32),
            pltpu.SemaphoreType.DMA((2, 4)),
        ],
        input_output_aliases={4 + k: k for k in range(len(outs))},
        cost_estimate=SHORT,
        compiler_params=PARAMS,
    )(spot, total, anchor, momentum, *outs)


def replica_sum(spot, ours, got, late):
    keep, send = pair_sum(spot, ours, got)
    total = add([keep, swap(send, 1, 0)])
    total = add([after(total, late), swap(total, 2, 0)])
    return join(spot, total, swap(total, 1, 0))


def on_device(
    anchor, first_moment, second_moment, outer_momentum, activations, cotangents, token_ids, exponents
):
    place = lax.axis_index("fsdp").astype(jnp.int32)
    z, x, y = place // PLANE, (place // NY) % NX, place % NY
    copy = lax.axis_index("replica").astype(jnp.int32)
    spot = jnp.stack([x, y, copy % CORES, copy // CORES, z])

    rings = ("y", "x")

    sent = [pack("y", 0, spot, token_ids, cotangents, activations)]
    sent.append(pack("x", 1, spot, token_ids, cotangents, activations))

    def gather(ahead, back, handed):
        ahead = [along(ring, block, 1) for ring, block in zip(rings, ahead)]
        back = [along(ring, block, -1) for ring, block in zip(rings, back)]
        on = [along(ring, block[-handed:], 1) for ring, block in zip(rings, ahead)]
        off = [along(ring, block[-handed:], -1) for ring, block in zip(rings, back)]
        return [[ahead[step], back[step], on[step], off[step]] for step in range(2)]

    def reduce(pieces, dtype):
        parts = []
        for ring, piece in zip(("x", "y"), pieces):
            low, high = opposite(piece)
            own, ahead, back = nearest(piece, along(ring, low, 1), along(ring, high, -1))
            parts += [own, along(ring, ahead, 1), along(ring, back, -1)]
        return totals(parts, dtype)

    soon = gather([block[1] for block in sent], [block[2] for block in sent], 4)
    soon = [[sent[step][0]] + soon[step] for step in range(2)]
    theirs = reduce(soon, jnp.bfloat16)
    got = lax.ppermute(theirs, "fsdp", fsdp_shift(1, 0, 0))
    late = gather([block[3] for block in sent], [block[4] for block in sent], 2)
    own = reduce([soon[step] + late[step] for step in range(2)], jnp.float32)

    state = anchor, first_moment, second_moment, own, got
    other = swap(code(1, spot, *state, exponents), 0, 1)
    keep = code(0, spot, *state, exponents)
    new_first, new_second = moments(*state[:4], after(got, other))
    total = replica_sum(spot, keep, other, new_first)
    other = swap(total, 0, 1)
    outs = outer_step(0, spot, total, anchor, outer_momentum)
    new_weights, new_momentum = outer_step(1, spot, other, anchor, outer_momentum, outs)
    return new_weights, new_momentum, new_first, new_second


def solution(mesh):
    in_specs = (
        P("fsdp", None),
        P("replica", "fsdp", None),
        P("replica", "fsdp", None),
        P("fsdp", None),
        P("replica", None, "fsdp", None),
        P("replica", None, "fsdp", None),
        P("replica", None, "fsdp"),
        P("replica", "fsdp", None),
    )
    out_specs = (
        P("fsdp", None),
        P("fsdp", None),
        P("replica", "fsdp", None),
        P("replica", "fsdp", None),
    )
    return jax.shard_map(
        on_device, mesh=mesh, in_specs=in_specs, out_specs=out_specs, check_vma=False
    )
```

```python
import functools

import jax
import jax.numpy as jnp
from jax import lax
from jax.experimental import pallas as pl
from jax.experimental.pallas import tpu as pltpu
from jax.sharding import PartitionSpec as P

BETA_ONE = 0.9
BETA_TWO = 0.95
EPSILON = 1e-08
INNER_RATE = 0.1
DECAY = 0.1
OUTER_RATE = 0.7
MOMENTUM = 0.9
CODE_LIMIT = 448.0
LOWEST = 13

NZ, NX, NY = 2, 4, 4
PLANE = NX * NY
LINE, CORES = 4, 2
LIMIT = 12 * 1024 * 1024

HBM = pl.BlockSpec(memory_space=pltpu.HBM)
VMEM = pl.BlockSpec(memory_space=pltpu.VMEM)
SMEM = pl.BlockSpec(memory_space=pltpu.SMEM)
PARAMS = pltpu.CompilerParams(vmem_limit_bytes=LIMIT)
SHORT = pl.CostEstimate(flops=1, bytes_accessed=1, transcendentals=0)


def fsdp_shift(dz, dx, dy):
    def at(z, x, y):
        return ((z % NZ) * NX + x % NX) * NY + y % NY

    return [
        (at(z, x, y), at(z + dz, x + dx, y + dy))
        for z in range(NZ)
        for x in range(NX)
        for y in range(NY)
    ]


def along(dim, block, turn):
    shift = (0, turn, 0) if dim == "x" else (0, 0, turn)
    return lax.ppermute(block, "fsdp", fsdp_shift(*shift))


def after(value, earlier):
    return lax.optimization_barrier((value, earlier))[0]


def shape_of(shape, dtype):
    return jax.ShapeDtypeStruct(shape, dtype)


def pack_kernel(dim, step, spot, ids, cotangents, features, own, ahead, back, ahead_late, back_late, *scratch):
    held, words, grads, sems = scratch
    tokens, shard = own.shape[1:]
    part = tokens // 4
    small = [
        pltpu.make_async_copy(ids, words, sems.at[4]),
        pltpu.make_async_copy(cotangents.at[0, step], grads, sems.at[5]),
    ]
    loads = []
    for q in range(4):
        rows = pl.ds(q * part, part)
        loads.append(pltpu.make_async_copy(features.at[0, step, rows], held.at[rows], sems.at[q]))
    for load in small + loads:
        load.start()
    for load in small:
        load.wait()
    live = jnp.sum((words[0, step : step + 1, :] != 0).astype(jnp.int32))
    alive = lax.broadcasted_iota(jnp.int32, (tokens, shard), 0) < live
    for n in range(4):
        block = grads[:, n * shard : (n + 1) * shard]
        block = jnp.where(alive, block, jnp.zeros_like(block))
        own[8 + n] = block
        ahead[4 + (n + 2) % 4] = block
        back[4 + n] = block
    x, y, z = spot[0], spot[1], spot[4]
    places = {}
    for u in range(4):
        for side, (to_ahead, to_back) in enumerate(((ahead, back), (ahead_late, back_late))):
            far = (to_ahead, to_back)[u // 2]
            places[side, 0, u] = own, 4 * side + u
            places[side, 1, u] = to_ahead, u
            places[side, 2, u] = far, far.shape[0] - 2 + u % 2
            places[side, 3, u] = to_back, u
    for q, load in enumerate(loads):
        load.wait()
        rows = slice(q * part, (q + 1) * part)
        for (side, turn, u), (out, slot) in places.items():
            to_x, to_y = (u, turn) if dim == "y" else (turn, u)
            owner = (lax.rem(z + 1 + side, NZ) * NX + lax.rem(x + to_x, NX)) * NY
            owner = owner + lax.rem(y + to_y, NY)
            at = pl.ds(pl.multiple_of(owner * shard, shard), shard)
            out[slot, rows, :] = held[rows, at]


def pack(dim, step, spot, ids, cotangents, features):
    tokens, rows = features.shape[2:]
    shard = rows // (NZ * NX * NY)
    return pl.pallas_call(
        functools.partial(pack_kernel, dim, step),
        in_specs=[SMEM, HBM, HBM, HBM],
        out_specs=[VMEM] * 5,
        out_shape=[shape_of((blocks, tokens, shard), features.dtype) for blocks in (12, 10, 10, 6, 6)],
        scratch_shapes=[
            pltpu.VMEM((tokens, rows), features.dtype),
            pltpu.VMEM(ids.shape, ids.dtype),
            pltpu.VMEM(cotangents.shape[2:], cotangents.dtype),
            pltpu.SemaphoreType.DMA((6,)),
        ],
        cost_estimate=SHORT,
        compiler_params=PARAMS,
    )(spot, ids, cotangents, features)


def products(turn, pieces):
    own, ahead, back = pieces[:3]
    handed = pieces[3:5]
    if len(pieces) == 5:
        left = [own[turn], ahead[turn], back[turn], handed[turn // 2][2 + turn % 2]]
    else:
        late = pieces[5:]
        left = [own[4 + turn], late[0][turn], late[1][turn], late[2 + turn // 2][turn % 2]]
    left = jnp.concatenate(left, axis=0)
    for n in range(4):
        right = [own[8 + n], ahead[4 + (n + 2) % 4], back[4 + n], handed[n // 2][n % 2]]
        yield n, lax.dot_general(
            left,
            jnp.concatenate(right, axis=0),
            (((0,), (0,)), ((), ())),
            preferred_element_type=jnp.float32,
        )


def opposite_kernel(*refs):
    pieces, (low, high) = refs[:-2], refs[-2:]
    shard, half = pieces[0].shape[2], low.shape[0]
    for n, value in products(2, pieces):
        low[:, n * shard : (n + 1) * shard] = value[:half].astype(low.dtype)
        high[:, n * shard : (n + 1) * shard] = value[half:].astype(high.dtype)


def opposite(pieces):
    _, _, shard = pieces[0].shape
    out = shape_of((shard // 2, 4 * shard), pieces[0].dtype)
    return pl.pallas_call(
        opposite_kernel, in_specs=[VMEM] * len(pieces), out_specs=[VMEM] * 2, out_shape=[out] * 2,
        cost_estimate=SHORT, compiler_params=PARAMS,
    )(*pieces)


def nearest_kernel(*refs):
    pieces, (low, high, own, ahead, back) = refs[:-5], refs[-5:]
    shard, half = pieces[0].shape[2], low.shape[0]
    for n, value in products(1, pieces):
        at = slice(n * shard, (n + 1) * shard)
        ahead[:half, at] = (value[:half] + low[:, at].astype(jnp.float32)).astype(ahead.dtype)
        ahead[half:, at] = value[half:].astype(ahead.dtype)
    for n, value in products(3, pieces):
        at = slice(n * shard, (n + 1) * shard)
        back[:half, at] = value[:half].astype(back.dtype)
        back[half:, at] = (value[half:] + high[:, at].astype(jnp.float32)).astype(back.dtype)
    for n, value in products(0, pieces):
        own[:, n * shard : (n + 1) * shard] = value


def nearest(pieces, low, high):
    _, _, shard = pieces[0].shape
    shape = (shard, 4 * shard)
    sent = shape_of(shape, pieces[0].dtype)
    return pl.pallas_call(
        nearest_kernel, in_specs=[VMEM] * (len(pieces) + 2), out_specs=[VMEM] * 3,
        out_shape=[shape_of(shape, jnp.float32), sent, sent],
        cost_estimate=SHORT, compiler_params=PARAMS,
    )(*pieces, low, high)


def total_kernel(*refs):
    ins, out = refs[:-1], refs[-1]

    @pl.loop(0, out.shape[1], step=16)
    def _(r):
        rows = pl.ds(pl.multiple_of(r, 16), 16)
        for step in range(out.shape[0]):
            total = ins[3 * step][rows, :]
            for ref in ins[3 * step + 1 : 3 * step + 3]:
                total = total + ref[rows, :].astype(jnp.float32)
            out[step, rows, :] = total.astype(out.dtype)


def totals(parts, dtype):
    return pl.pallas_call(
        total_kernel, in_specs=[VMEM] * len(parts), out_specs=VMEM,
        out_shape=shape_of((len(parts) // 3,) + parts[0].shape, dtype),
        cost_estimate=SHORT, compiler_params=PARAMS,
    )(*parts)


def add_kernel(*refs):
    total = refs[0][...].astype(jnp.float32)
    for ref in refs[1:-1]:
        total = total + ref[...].astype(jnp.float32)
    refs[-1][...] = total.astype(refs[-1].dtype)


def add(parts):
    return pl.pallas_call(
        add_kernel, in_specs=[VMEM] * len(parts), out_specs=VMEM,
        out_shape=shape_of(parts[0].shape, parts[0].dtype), cost_estimate=SHORT, compiler_params=PARAMS,
    )(*parts)


def adam_update(weights, first, second, gradient):
    first = BETA_ONE * first + (1.0 - BETA_ONE) * gradient
    second = BETA_TWO * second + (1.0 - BETA_TWO) * gradient * gradient
    root = second * lax.rsqrt(second)
    weights = weights - INNER_RATE * (first / (root + EPSILON) + DECAY * weights)
    return weights, first, second


def inner_steps(anchor, first, second, own, got, here):
    weights, one, two = anchor[here], first[(0,) + here], second[(0,) + here]
    for step, ref in enumerate(own):
        gradient = ref[(0,) + here] + got[(step,) + here].astype(jnp.float32)
        weights, one, two = adam_update(weights, one, two, gradient)
    return weights, one, two


def code_kernel(turn, spot, anchor, first, second, own_a, own_b, got, scale, out):
    own = own_a, own_b
    half = out.shape[0]
    base = lax.rem(spot[2] + turn, CORES) * half

    @pl.loop(0, half, step=16)
    def _(r):
        rows = pl.ds(pl.multiple_of(base + r, 16), 16)
        for c in range(0, anchor.shape[1], 256):
            here = (rows, pl.ds(c, 256))
            delta = anchor[here] - inner_steps(anchor, first, second, own, got, here)[0]
            for block in range(2):
                at = c // 128 + block
                power = jnp.broadcast_to(scale[0, rows, at : at + 1], (16, 128))
                ones = jnp.ones_like(power)
                factor = jnp.left_shift(ones, -power).astype(jnp.float32)
                back = jnp.left_shift(ones, power + LOWEST).astype(jnp.float32) * 2.0**-LOWEST
                coded = delta[:, block * 128 : (block + 1) * 128] * factor
                coded = jnp.clip(coded, -CODE_LIMIT, CODE_LIMIT).astype(jnp.bfloat16)
                out[pl.ds(pl.multiple_of(r, 16), 16), pl.ds(at * 128, 128)] = (
                    coded.astype(jnp.float32) * back
                ).astype(jnp.bfloat16)


def code(turn, spot, anchor, first, second, own, got, exponents):
    rows, width = anchor.shape
    return pl.pallas_call(
        functools.partial(code_kernel, turn),
        in_specs=[SMEM] + [VMEM] * 7, out_specs=VMEM,
        out_shape=shape_of((rows // CORES, width), jnp.bfloat16),
        cost_estimate=SHORT, compiler_params=PARAMS,
    )(spot, anchor, first, second, *own, got, exponents)


def moment_kernel(anchor, first, second, own_a, own_b, got, new_first, new_second):
    own = own_a, own_b

    @pl.loop(0, anchor.shape[0], step=16)
    def _(r):
        rows = pl.ds(pl.multiple_of(r, 16), 16)
        for c in range(0, anchor.shape[1], 256):
            here = (rows, pl.ds(c, 256))
            _, one, two = inner_steps(anchor, first, second, own, got, here)
            new_first[(0,) + here] = one
            new_second[(0,) + here] = two


def moments(anchor, first, second, own, got):
    out = shape_of(first.shape, first.dtype)
    return pl.pallas_call(
        moment_kernel, in_specs=[VMEM] * 6, out_specs=[VMEM] * 2, out_shape=[out] * 2,
        cost_estimate=SHORT, compiler_params=PARAMS,
    )(anchor, first, second, *own, got)


def pair_kernel(spot, ours, got, keep, send):
    rows = keep.shape[0]
    for turn, out in ((1, send), (0, keep)):
        at = pl.ds(pl.multiple_of(lax.rem(spot[3] + turn, 2) * rows, rows), rows)
        total = ours[at, :].astype(jnp.float32) + got[at, :].astype(jnp.float32)
        out[...] = total.astype(out.dtype)


def pair_sum(spot, ours, got):
    rows, width = ours.shape
    out = shape_of((rows // 2, width), ours.dtype)
    return pl.pallas_call(
        pair_kernel, in_specs=[SMEM, VMEM, VMEM], out_specs=[VMEM] * 2, out_shape=[out] * 2,
        cost_estimate=SHORT, compiler_params=PARAMS,
    )(spot, ours, got)


def swap(block, line, core):
    pairs = [
        (z * CORES + c, (z ^ line) * CORES + (c ^ core)) for z in range(LINE) for c in range(CORES)
    ]
    return lax.ppermute(block, "replica", pairs)


def outer_kernel(turns, spot, anchor, momentum, *refs):
    totals, (new_weights, new_momentum, weights, moving, sems) = refs[: len(turns)], refs[-5:]
    rows = totals[0].shape[0]
    stores = []
    for part, ((core, line), total) in enumerate(zip(turns, totals)):
        quarter = lax.rem(spot[2] + core, CORES) * 2 + lax.rem(spot[3] + line, 2)
        tile = rows // 2
        for r in range(0, rows, tile):
            here = pl.ds(pl.multiple_of(quarter * rows + r, tile), tile)
            average = total[r : r + tile, :].astype(jnp.float32) * (1.0 / (LINE * CORES))
            moved = MOMENTUM * momentum[here, :] + average
            moving[part, r : r + tile, :] = moved
            weights[part, r : r + tile, :] = anchor[here, :] - OUTER_RATE * (average + MOMENTUM * moved)
            for k, (held, out) in enumerate(((moving, new_momentum), (weights, new_weights))):
                store = pltpu.make_async_copy(
                    held.at[part, pl.ds(r, tile)], out.at[here], sems.at[k, part, r // tile]
                )
                store.start()
                stores.append(store)
    for store in stores:
        store.wait()


def outer_step(turns, spot, anchor, momentum, totals, outs=()):
    count, (rows, width) = len(turns), totals[0].shape
    return pl.pallas_call(
        functools.partial(outer_kernel, turns),
        in_specs=[SMEM] + [VMEM] * (2 + count) + [HBM] * len(outs),
        out_specs=[HBM] * 2,
        out_shape=[shape_of(anchor.shape, anchor.dtype)] * 2,
        scratch_shapes=[
            pltpu.VMEM((count, rows, width), jnp.float32),
            pltpu.VMEM((count, rows, width), jnp.float32),
            pltpu.SemaphoreType.DMA((2, count, 2)),
        ],
        input_output_aliases={3 + count + k: k for k in range(len(outs))},
        cost_estimate=SHORT,
        compiler_params=PARAMS,
    )(spot, anchor, momentum, *totals, *outs)


def on_device(
    anchor, first_moment, second_moment, outer_momentum, activations, cotangents, token_ids, exponents
):
    place = lax.axis_index("fsdp").astype(jnp.int32)
    z, x, y = place // PLANE, (place // NY) % NX, place % NY
    copy = lax.axis_index("replica").astype(jnp.int32)
    spot = jnp.stack([x, y, copy % CORES, copy // CORES, z])

    rings = ("y", "x")

    sent = [pack("y", 0, spot, token_ids, cotangents, activations)]
    sent.append(pack("x", 1, spot, token_ids, cotangents, activations))

    def gather(ahead, back, handed):
        ahead = [along(ring, block, 1) for ring, block in zip(rings, ahead)]
        back = [along(ring, block, -1) for ring, block in zip(rings, back)]
        on = [along(ring, block[-handed:], 1) for ring, block in zip(rings, ahead)]
        off = [along(ring, block[-handed:], -1) for ring, block in zip(rings, back)]
        return [[ahead[step], back[step], on[step], off[step]] for step in range(2)]

    def reduce(pieces):
        parts = []
        for ring, piece in zip(("x", "y"), pieces):
            low, high = opposite(piece)
            own, ahead, back = nearest(piece, along(ring, low, 1), along(ring, high, -1))
            parts.append([own, along(ring, ahead, 1), along(ring, back, -1)])
        return parts

    soon = gather([block[1] for block in sent], [block[2] for block in sent], 4)
    soon = [[sent[step][0]] + soon[step] for step in range(2)]
    theirs = totals(sum(reduce(soon), []), jnp.bfloat16)
    got = lax.ppermute(theirs, "fsdp", fsdp_shift(1, 0, 0))
    late = gather([block[3] for block in sent], [block[4] for block in sent], 2)
    own = [totals(part, jnp.float32) for part in reduce([soon[step] + late[step] for step in range(2)])]

    state = anchor, first_moment, second_moment, own, got
    other = swap(code(1, spot, *state, exponents), 0, 1)
    keep = code(0, spot, *state, exponents)
    new_first, new_second = moments(*state[:4], after(got, other))
    kept, sent = pair_sum(spot, keep, other)
    total = add([kept, swap(sent, 1, 0)])
    total = add([after(total, new_first), swap(total, 2, 0)])
    across = swap(total, 0, 1)
    beside = swap(total, 1, 0)
    outs = outer_step([(0, 0)], spot, anchor, outer_momentum, [total])
    last = swap(after(beside, outs), 0, 1)
    outs = outer_step([(0, 1), (1, 0)], spot, anchor, outer_momentum, [beside, across], outs)
    new_weights, new_momentum = outer_step([(1, 1)], spot, anchor, outer_momentum, [last], outs)
    return new_weights, new_momentum, new_first, new_second


def solution(mesh):
    in_specs = (
        P("fsdp", None),
        P("replica", "fsdp", None),
        P("replica", "fsdp", None),
        P("fsdp", None),
        P("replica", None, "fsdp", None),
        P("replica", None, "fsdp", None),
        P("replica", None, "fsdp"),
        P("replica", "fsdp", None),
    )
    out_specs = (
        P("fsdp", None),
        P("fsdp", None),
        P("replica", "fsdp", None),
        P("replica", "fsdp", None),
    )
    return jax.shard_map(
        on_device, mesh=mesh, in_specs=in_specs, out_specs=out_specs, check_vma=False
    )
```

```python
import functools

import jax
import jax.numpy as jnp
from jax import lax
from jax.experimental import pallas as pl
from jax.experimental.pallas import tpu as pltpu
from jax.sharding import PartitionSpec as P

BETA_ONE = 0.9
BETA_TWO = 0.95
EPSILON = 1e-08
INNER_RATE = 0.1
DECAY = 0.1
OUTER_RATE = 0.7
MOMENTUM = 0.9
CODE_LIMIT = 448.0
LOWEST = 13

NZ, NX, NY = 2, 4, 4
PLANE = NX * NY
LINE, CORES = 4, 2
LIMIT = 12 * 1024 * 1024

HBM = pl.BlockSpec(memory_space=pltpu.HBM)
VMEM = pl.BlockSpec(memory_space=pltpu.VMEM)
SMEM = pl.BlockSpec(memory_space=pltpu.SMEM)
PARAMS = pltpu.CompilerParams(vmem_limit_bytes=LIMIT)
SHORT = pl.CostEstimate(flops=1, bytes_accessed=1, transcendentals=0)


def fsdp_shift(dz, dx, dy):
    def at(z, x, y):
        return ((z % NZ) * NX + x % NX) * NY + y % NY

    return [
        (at(z, x, y), at(z + dz, x + dx, y + dy))
        for z in range(NZ)
        for x in range(NX)
        for y in range(NY)
    ]


def along(dim, block, turn):
    shift = (0, turn, 0) if dim == "x" else (0, 0, turn)
    return lax.ppermute(block, "fsdp", fsdp_shift(*shift))


def after(value, earlier):
    return lax.optimization_barrier((value, earlier))[0]


def shape_of(shape, dtype):
    return jax.ShapeDtypeStruct(shape, dtype)


def pack_kernel(dim, step, spot, cotangents, features, own, ahead, back, ahead_late, back_late, *scratch):
    held, grads, sems = scratch
    tokens, shard = own.shape[1:]
    part = tokens // 4
    small = pltpu.make_async_copy(cotangents.at[0, step], grads, sems.at[4])
    loads = []
    for q in range(4):
        rows = pl.ds(q * part, part)
        loads.append(pltpu.make_async_copy(features.at[0, step, rows], held.at[rows], sems.at[q]))
    for load in [small] + loads:
        load.start()
    small.wait()
    alive = lax.broadcasted_iota(jnp.int32, (tokens, shard), 0) < spot[5 + step]
    for n in range(4):
        block = grads[:, n * shard : (n + 1) * shard]
        block = jnp.where(alive, block, jnp.zeros_like(block))
        own[8 + n] = block
        ahead[4 + (n + 2) % 4] = block
        back[4 + n] = block
    x, y, z = spot[0], spot[1], spot[4]
    places = {}
    for u in range(4):
        for side, (to_ahead, to_back) in enumerate(((ahead, back), (ahead_late, back_late))):
            far = (to_ahead, to_back)[u // 2]
            places[side, 0, u] = own, 4 * side + u
            places[side, 1, u] = to_ahead, u
            places[side, 2, u] = far, far.shape[0] - 2 + u % 2
            places[side, 3, u] = to_back, u
    for q, load in enumerate(loads):
        load.wait()
        rows = slice(q * part, (q + 1) * part)
        for (side, turn, u), (out, slot) in places.items():
            to_x, to_y = (u, turn) if dim == "y" else (turn, u)
            owner = (lax.rem(z + 1 + side, NZ) * NX + lax.rem(x + to_x, NX)) * NY
            owner = owner + lax.rem(y + to_y, NY)
            at = pl.ds(pl.multiple_of(owner * shard, shard), shard)
            out[slot, rows, :] = held[rows, at]


def pack(dim, step, spot, cotangents, features):
    tokens, rows = features.shape[2:]
    shard = rows // (NZ * NX * NY)
    return pl.pallas_call(
        functools.partial(pack_kernel, dim, step),
        in_specs=[SMEM, HBM, HBM],
        out_specs=[VMEM] * 5,
        out_shape=[shape_of((blocks, tokens, shard), features.dtype) for blocks in (12, 10, 10, 6, 6)],
        scratch_shapes=[
            pltpu.VMEM((tokens, rows), features.dtype),
            pltpu.VMEM(cotangents.shape[2:], cotangents.dtype),
            pltpu.SemaphoreType.DMA((5,)),
        ],
        cost_estimate=SHORT,
        compiler_params=PARAMS,
    )(spot, cotangents, features)


def products(turn, pieces):
    own, ahead, back = pieces[:3]
    handed = pieces[3:5]
    if len(pieces) == 5:
        left = [own[turn], ahead[turn], back[turn], handed[turn // 2][2 + turn % 2]]
    else:
        late = pieces[5:]
        left = [own[4 + turn], late[0][turn], late[1][turn], late[2 + turn // 2][turn % 2]]
    left = jnp.concatenate(left, axis=0)
    for n in range(4):
        right = [own[8 + n], ahead[4 + (n + 2) % 4], back[4 + n], handed[n // 2][n % 2]]
        yield n, lax.dot_general(
            left,
            jnp.concatenate(right, axis=0),
            (((0,), (0,)), ((), ())),
            preferred_element_type=jnp.float32,
        )


def opposite_kernel(*refs):
    pieces, (low, high) = refs[:-2], refs[-2:]
    shard, half = pieces[0].shape[2], low.shape[0]
    for n, value in products(2, pieces):
        low[:, n * shard : (n + 1) * shard] = value[:half].astype(low.dtype)
        high[:, n * shard : (n + 1) * shard] = value[half:].astype(high.dtype)


def opposite(pieces):
    _, _, shard = pieces[0].shape
    out = shape_of((shard // 2, 4 * shard), pieces[0].dtype)
    return pl.pallas_call(
        opposite_kernel, in_specs=[VMEM] * len(pieces), out_specs=[VMEM] * 2, out_shape=[out] * 2,
        cost_estimate=SHORT, compiler_params=PARAMS,
    )(*pieces)


def nearest_kernel(*refs):
    pieces, (low, high, ahead, back) = refs[:-4], refs[-4:]
    shard, half = pieces[0].shape[2], low.shape[0]
    for n, value in products(1, pieces):
        at = slice(n * shard, (n + 1) * shard)
        ahead[:half, at] = (value[:half] + low[:, at].astype(jnp.float32)).astype(ahead.dtype)
        ahead[half:, at] = value[half:].astype(ahead.dtype)
    for n, value in products(3, pieces):
        at = slice(n * shard, (n + 1) * shard)
        back[:half, at] = value[:half].astype(back.dtype)
        back[half:, at] = (value[half:] + high[:, at].astype(jnp.float32)).astype(back.dtype)


def nearest(pieces, low, high):
    _, _, shard = pieces[0].shape
    out = shape_of((shard, 4 * shard), pieces[0].dtype)
    return pl.pallas_call(
        nearest_kernel, in_specs=[VMEM] * (len(pieces) + 2), out_specs=[VMEM] * 2, out_shape=[out] * 2,
        cost_estimate=SHORT, compiler_params=PARAMS,
    )(*pieces, low, high)


def itself_kernel(*refs):
    pieces, out = refs[:-1], refs[-1]
    shard = pieces[0].shape[2]
    for n, value in products(0, pieces):
        out[:, n * shard : (n + 1) * shard] = value


def itself(pieces):
    _, _, shard = pieces[0].shape
    return pl.pallas_call(
        itself_kernel, in_specs=[VMEM] * len(pieces), out_specs=VMEM,
        out_shape=shape_of((shard, 4 * shard), jnp.float32),
        cost_estimate=SHORT, compiler_params=PARAMS,
    )(*pieces)


def total_kernel(*refs):
    ins, out = refs[:-1], refs[-1]

    @pl.loop(0, out.shape[1], step=16)
    def _(r):
        rows = pl.ds(pl.multiple_of(r, 16), 16)
        for step in range(out.shape[0]):
            total = ins[3 * step][rows, :]
            for ref in ins[3 * step + 1 : 3 * step + 3]:
                total = total + ref[rows, :].astype(jnp.float32)
            out[step, rows, :] = total.astype(out.dtype)


def totals(parts, dtype):
    return pl.pallas_call(
        total_kernel, in_specs=[VMEM] * len(parts), out_specs=VMEM,
        out_shape=shape_of((len(parts) // 3,) + parts[0].shape, dtype),
        cost_estimate=SHORT, compiler_params=PARAMS,
    )(*parts)


def add_kernel(*refs):
    total = refs[0][...].astype(jnp.float32)
    for ref in refs[1:-1]:
        total = total + ref[...].astype(jnp.float32)
    refs[-1][...] = total.astype(refs[-1].dtype)


def add(parts):
    return pl.pallas_call(
        add_kernel, in_specs=[VMEM] * len(parts), out_specs=VMEM,
        out_shape=shape_of(parts[0].shape, parts[0].dtype), cost_estimate=SHORT, compiler_params=PARAMS,
    )(*parts)


def adam_update(weights, first, second, gradient):
    first = BETA_ONE * first + (1.0 - BETA_ONE) * gradient
    second = BETA_TWO * second + (1.0 - BETA_TWO) * gradient * gradient
    root = second * lax.rsqrt(second)
    weights = weights - INNER_RATE * (first / (root + EPSILON) + DECAY * weights)
    return weights, first, second


def inner_steps(anchor, first, second, own, got, here):
    weights, one, two = anchor[here], first[(0,) + here], second[(0,) + here]
    for step, ref in enumerate(own):
        gradient = ref[(0,) + here] + got[(step,) + here].astype(jnp.float32)
        weights, one, two = adam_update(weights, one, two, gradient)
    return weights, one, two


def code_kernel(turn, spot, anchor, first, second, own_a, own_b, got, scale, out):
    own = own_a, own_b
    half = out.shape[0]
    base = lax.rem(spot[2] + turn, CORES) * half

    @pl.loop(0, half, step=16, unroll=2)
    def _(r):
        rows = pl.ds(pl.multiple_of(base + r, 16), 16)
        for c in range(0, anchor.shape[1], 256):
            here = (rows, pl.ds(c, 256))
            delta = anchor[here] - inner_steps(anchor, first, second, own, got, here)[0]
            for block in range(2):
                at = c // 128 + block
                power = jnp.broadcast_to(scale[0, rows, at : at + 1], (16, 128))
                ones = jnp.ones_like(power)
                factor = jnp.left_shift(ones, -power).astype(jnp.float32)
                back = jnp.left_shift(ones, power + LOWEST).astype(jnp.float32) * 2.0**-LOWEST
                coded = delta[:, block * 128 : (block + 1) * 128] * factor
                coded = jnp.clip(coded, -CODE_LIMIT, CODE_LIMIT).astype(jnp.bfloat16)
                out[pl.ds(pl.multiple_of(r, 16), 16), pl.ds(at * 128, 128)] = (
                    coded.astype(jnp.float32) * back
                ).astype(jnp.bfloat16)


def code(turn, spot, anchor, first, second, own, got, exponents):
    rows, width = anchor.shape
    return pl.pallas_call(
        functools.partial(code_kernel, turn),
        in_specs=[SMEM] + [VMEM] * 7, out_specs=VMEM,
        out_shape=shape_of((rows // CORES, width), jnp.bfloat16),
        cost_estimate=SHORT, compiler_params=PARAMS,
    )(spot, anchor, first, second, *own, got, exponents)


def moment_kernel(anchor, first, second, own_a, own_b, got, new_first, new_second):
    own = own_a, own_b

    @pl.loop(0, anchor.shape[0], step=16)
    def _(r):
        rows = pl.ds(pl.multiple_of(r, 16), 16)
        for c in range(0, anchor.shape[1], 256):
            here = (rows, pl.ds(c, 256))
            _, one, two = inner_steps(anchor, first, second, own, got, here)
            new_first[(0,) + here] = one
            new_second[(0,) + here] = two


def moments(anchor, first, second, own, got):
    out = shape_of(first.shape, first.dtype)
    return pl.pallas_call(
        moment_kernel, in_specs=[VMEM] * 6, out_specs=[VMEM] * 2, out_shape=[out] * 2,
        cost_estimate=SHORT, compiler_params=PARAMS,
    )(anchor, first, second, *own, got)


def pair_kernel(spot, ours, got, keep, send):
    rows = keep.shape[0]
    for turn, out in ((1, send), (0, keep)):
        at = pl.ds(pl.multiple_of(lax.rem(spot[3] + turn, 2) * rows, rows), rows)
        total = ours[at, :].astype(jnp.float32) + got[at, :].astype(jnp.float32)
        out[...] = total.astype(out.dtype)


def pair_sum(spot, ours, got):
    rows, width = ours.shape
    out = shape_of((rows // 2, width), ours.dtype)
    return pl.pallas_call(
        pair_kernel, in_specs=[SMEM, VMEM, VMEM], out_specs=[VMEM] * 2, out_shape=[out] * 2,
        cost_estimate=SHORT, compiler_params=PARAMS,
    )(spot, ours, got)


def swap(block, line, core):
    pairs = [
        (z * CORES + c, (z ^ line) * CORES + (c ^ core)) for z in range(LINE) for c in range(CORES)
    ]
    return lax.ppermute(block, "replica", pairs)


def outer_kernel(turns, spot, anchor, momentum, *refs):
    totals, (new_weights, new_momentum, weights, moving, sems) = refs[: len(turns)], refs[-5:]
    rows = totals[0].shape[0]
    stores = []
    for part, ((core, line), total) in enumerate(zip(turns, totals)):
        quarter = lax.rem(spot[2] + core, CORES) * 2 + lax.rem(spot[3] + line, 2)
        tile = rows // 2
        for r in range(0, rows, tile):
            here = pl.ds(pl.multiple_of(quarter * rows + r, tile), tile)
            average = total[r : r + tile, :].astype(jnp.float32) * (1.0 / (LINE * CORES))
            moved = MOMENTUM * momentum[here, :] + average
            moving[part, r : r + tile, :] = moved
            weights[part, r : r + tile, :] = anchor[here, :] - OUTER_RATE * (average + MOMENTUM * moved)
            for k, (held, out) in enumerate(((moving, new_momentum), (weights, new_weights))):
                store = pltpu.make_async_copy(
                    held.at[part, pl.ds(r, tile)], out.at[here], sems.at[k, part, r // tile]
                )
                store.start()
                stores.append(store)
    for store in stores:
        store.wait()


def outer_step(turns, spot, anchor, momentum, totals, outs=()):
    count, (rows, width) = len(turns), totals[0].shape
    return pl.pallas_call(
        functools.partial(outer_kernel, turns),
        in_specs=[SMEM] + [VMEM] * (2 + count) + [HBM] * len(outs),
        out_specs=[HBM] * 2,
        out_shape=[shape_of(anchor.shape, anchor.dtype)] * 2,
        scratch_shapes=[
            pltpu.VMEM((count, rows, width), jnp.float32),
            pltpu.VMEM((count, rows, width), jnp.float32),
            pltpu.SemaphoreType.DMA((2, count, 2)),
        ],
        input_output_aliases={3 + count + k: k for k in range(len(outs))},
        cost_estimate=SHORT,
        compiler_params=PARAMS,
    )(spot, anchor, momentum, *totals, *outs)


def on_device(
    anchor, first_moment, second_moment, outer_momentum, activations, cotangents, token_ids, exponents
):
    place = lax.axis_index("fsdp").astype(jnp.int32)
    z, x, y = place // PLANE, (place // NY) % NX, place % NY
    copy = lax.axis_index("replica").astype(jnp.int32)
    live = jnp.sum((token_ids[0] != 0).astype(jnp.int32), axis=1)
    spot = jnp.stack([x, y, copy % CORES, copy // CORES, z, live[0], live[1]])

    rings = ("y", "x")

    sent = [pack("y", 0, spot, cotangents, activations)]
    sent.append(pack("x", 1, spot, cotangents, activations))

    def gather(ahead, back, handed):
        ahead = [along(ring, block, 1) for ring, block in zip(rings, ahead)]
        back = [along(ring, block, -1) for ring, block in zip(rings, back)]
        on = [along(ring, block[-handed:], 1) for ring, block in zip(rings, ahead)]
        off = [along(ring, block[-handed:], -1) for ring, block in zip(rings, back)]
        return [[ahead[step], back[step], on[step], off[step]] for step in range(2)]

    def reduce(pieces):
        parts = []
        for ring, piece in zip(("x", "y"), pieces):
            low, high = opposite(piece)
            low, high = along(ring, low, 1), along(ring, high, -1)
            own = itself(piece)
            ahead, back = nearest(piece, low, after(high, own))
            parts.append([own, along(ring, ahead, 1), along(ring, back, -1)])
        return parts

    soon = gather([block[1] for block in sent], [block[2] for block in sent], 4)
    soon = [[sent[step][0]] + soon[step] for step in range(2)]
    theirs = totals(sum(reduce(soon), []), jnp.bfloat16)
    got = lax.ppermute(theirs, "fsdp", fsdp_shift(1, 0, 0))
    late = gather([block[3] for block in sent], [block[4] for block in sent], 2)
    own = [totals(part, jnp.float32) for part in reduce([soon[step] + late[step] for step in range(2)])]

    state = anchor, first_moment, second_moment, own, got
    other = swap(code(1, spot, *state, exponents), 0, 1)
    keep = code(0, spot, *state, exponents)
    new_first, new_second = moments(*state[:4], after(got, other))
    kept, sent = pair_sum(spot, keep, other)
    total = add([kept, swap(sent, 1, 0)])
    total = add([after(total, new_first), swap(total, 2, 0)])
    across = swap(total, 0, 1)
    beside = swap(total, 1, 0)
    outs = outer_step([(0, 0)], spot, anchor, outer_momentum, [total])
    last = swap(after(beside, outs), 0, 1)
    outs = outer_step([(0, 1), (1, 0)], spot, anchor, outer_momentum, [beside, across], outs)
    new_weights, new_momentum = outer_step([(1, 1)], spot, anchor, outer_momentum, [last], outs)
    return new_weights, new_momentum, new_first, new_second


def solution(mesh):
    in_specs = (
        P("fsdp", None),
        P("replica", "fsdp", None),
        P("replica", "fsdp", None),
        P("fsdp", None),
        P("replica", None, "fsdp", None),
        P("replica", None, "fsdp", None),
        P("replica", None, "fsdp"),
        P("replica", "fsdp", None),
    )
    out_specs = (
        P("fsdp", None),
        P("fsdp", None),
        P("replica", "fsdp", None),
        P("replica", "fsdp", None),
    )
    return jax.shard_map(
        on_device, mesh=mesh, in_specs=in_specs, out_specs=out_specs, check_vma=False
    )
```

```python
import functools

import jax
import jax.numpy as jnp
from jax import lax
from jax.experimental import pallas as pl
from jax.experimental.pallas import tpu as pltpu
from jax.sharding import PartitionSpec as P

BETA_ONE = 0.9
BETA_TWO = 0.95
EPSILON = 1e-08
INNER_RATE = 0.1
DECAY = 0.1
OUTER_RATE = 0.7
MOMENTUM = 0.9
CODE_LIMIT = 448.0
LOWEST = 13

NZ, NX, NY = 2, 4, 4
PLANE = NX * NY
LINE, CORES = 4, 2
LIMIT = 12 * 1024 * 1024

HBM = pl.BlockSpec(memory_space=pltpu.HBM)
VMEM = pl.BlockSpec(memory_space=pltpu.VMEM)
SMEM = pl.BlockSpec(memory_space=pltpu.SMEM)
PARAMS = pltpu.CompilerParams(vmem_limit_bytes=LIMIT)
SHORT = pl.CostEstimate(flops=1, bytes_accessed=1, transcendentals=0)


def fsdp_shift(dz, dx, dy):
    def at(z, x, y):
        return ((z % NZ) * NX + x % NX) * NY + y % NY

    return [
        (at(z, x, y), at(z + dz, x + dx, y + dy))
        for z in range(NZ)
        for x in range(NX)
        for y in range(NY)
    ]


def along(dim, block, turn):
    shift = (0, turn, 0) if dim == "x" else (0, 0, turn)
    return lax.ppermute(block, "fsdp", fsdp_shift(*shift))


def after(value, earlier):
    return lax.optimization_barrier((value, earlier))[0]


def shape_of(shape, dtype):
    return jax.ShapeDtypeStruct(shape, dtype)


def pack_kernel(dim, step, spot, cotangents, features, own, ahead, back, ahead_late, back_late, *scratch):
    held, grads, sems = scratch
    tokens, shard = own.shape[1:]
    part = tokens // 4
    small = pltpu.make_async_copy(cotangents.at[0, step], grads, sems.at[4])
    loads = []
    for q in range(4):
        rows = pl.ds(q * part, part)
        loads.append(pltpu.make_async_copy(features.at[0, step, rows], held.at[rows], sems.at[q]))
    for load in [small] + loads:
        load.start()
    small.wait()
    alive = lax.broadcasted_iota(jnp.int32, (tokens, shard), 0) < spot[5 + step]
    for n in range(4):
        block = grads[:, n * shard : (n + 1) * shard]
        block = jnp.where(alive, block, jnp.zeros_like(block))
        own[8 + n] = block
        ahead[4 + (n + 2) % 4] = block
        back[4 + n] = block
    x, y, z = spot[0], spot[1], spot[4]
    places = {}
    for u in range(4):
        for side, (to_ahead, to_back) in enumerate(((ahead, back), (ahead_late, back_late))):
            far = (to_ahead, to_back)[u // 2]
            places[side, 0, u] = own, 4 * side + u
            places[side, 1, u] = to_ahead, u
            places[side, 2, u] = far, far.shape[0] - 2 + u % 2
            places[side, 3, u] = to_back, u
    for q, load in enumerate(loads):
        load.wait()
        rows = slice(q * part, (q + 1) * part)
        for (side, turn, u), (out, slot) in places.items():
            to_x, to_y = (u, turn) if dim == "y" else (turn, u)
            owner = (lax.rem(z + 1 + side, NZ) * NX + lax.rem(x + to_x, NX)) * NY
            owner = owner + lax.rem(y + to_y, NY)
            at = pl.ds(pl.multiple_of(owner * shard, shard), shard)
            out[slot, rows, :] = held[rows, at]


def pack(dim, step, spot, cotangents, features):
    tokens, rows = features.shape[2:]
    shard = rows // (NZ * NX * NY)
    return pl.pallas_call(
        functools.partial(pack_kernel, dim, step),
        in_specs=[SMEM, HBM, HBM],
        out_specs=[VMEM] * 5,
        out_shape=[shape_of((blocks, tokens, shard), features.dtype) for blocks in (12, 10, 10, 6, 6)],
        scratch_shapes=[
            pltpu.VMEM((tokens, rows), features.dtype),
            pltpu.VMEM(cotangents.shape[2:], cotangents.dtype),
            pltpu.SemaphoreType.DMA((5,)),
        ],
        cost_estimate=SHORT,
        compiler_params=PARAMS,
    )(spot, cotangents, features)


def products(turn, pieces):
    own, ahead, back = pieces[:3]
    handed = pieces[3:5]
    if len(pieces) == 5:
        left = [own[turn], ahead[turn], back[turn], handed[turn // 2][2 + turn % 2]]
    else:
        late = pieces[5:]
        left = [own[4 + turn], late[0][turn], late[1][turn], late[2 + turn // 2][turn % 2]]
    left = jnp.concatenate(left, axis=0)
    for n in range(4):
        right = [own[8 + n], ahead[4 + (n + 2) % 4], back[4 + n], handed[n // 2][n % 2]]
        yield n, lax.dot_general(
            left,
            jnp.concatenate(right, axis=0),
            (((0,), (0,)), ((), ())),
            preferred_element_type=jnp.float32,
        )


def opposite_kernel(*refs):
    pieces, (low, high) = refs[:-2], refs[-2:]
    shard, half = pieces[0].shape[2], low.shape[0]
    for n, value in products(2, pieces):
        low[:, n * shard : (n + 1) * shard] = value[:half].astype(low.dtype)
        high[:, n * shard : (n + 1) * shard] = value[half:].astype(high.dtype)


def opposite(pieces):
    _, _, shard = pieces[0].shape
    out = shape_of((shard // 2, 4 * shard), pieces[0].dtype)
    return pl.pallas_call(
        opposite_kernel, in_specs=[VMEM] * len(pieces), out_specs=[VMEM] * 2, out_shape=[out] * 2,
        cost_estimate=SHORT, compiler_params=PARAMS,
    )(*pieces)


def nearest_kernel(*refs):
    pieces, (low, high, ahead, back) = refs[:-4], refs[-4:]
    shard, half = pieces[0].shape[2], low.shape[0]
    for n, value in products(1, pieces):
        at = slice(n * shard, (n + 1) * shard)
        ahead[:half, at] = (value[:half] + low[:, at].astype(jnp.float32)).astype(ahead.dtype)
        ahead[half:, at] = value[half:].astype(ahead.dtype)
    for n, value in products(3, pieces):
        at = slice(n * shard, (n + 1) * shard)
        back[:half, at] = value[:half].astype(back.dtype)
        back[half:, at] = (value[half:] + high[:, at].astype(jnp.float32)).astype(back.dtype)


def nearest(pieces, low, high):
    _, _, shard = pieces[0].shape
    out = shape_of((shard, 4 * shard), pieces[0].dtype)
    return pl.pallas_call(
        nearest_kernel, in_specs=[VMEM] * (len(pieces) + 2), out_specs=[VMEM] * 2, out_shape=[out] * 2,
        cost_estimate=SHORT, compiler_params=PARAMS,
    )(*pieces, low, high)


def itself_kernel(*refs):
    pieces, out = refs[:-1], refs[-1]
    shard = pieces[0].shape[2]
    for n, value in products(0, pieces):
        out[:, n * shard : (n + 1) * shard] = value


def itself(pieces):
    _, _, shard = pieces[0].shape
    return pl.pallas_call(
        itself_kernel, in_specs=[VMEM] * len(pieces), out_specs=VMEM,
        out_shape=shape_of((shard, 4 * shard), jnp.float32),
        cost_estimate=SHORT, compiler_params=PARAMS,
    )(*pieces)


def total_kernel(*refs):
    ins, out = refs[:-1], refs[-1]

    @pl.loop(0, out.shape[1], step=16)
    def _(r):
        rows = pl.ds(pl.multiple_of(r, 16), 16)
        for step in range(out.shape[0]):
            total = ins[3 * step][rows, :]
            for ref in ins[3 * step + 1 : 3 * step + 3]:
                total = total + ref[rows, :].astype(jnp.float32)
            out[step, rows, :] = total.astype(out.dtype)


def totals(parts, dtype):
    return pl.pallas_call(
        total_kernel, in_specs=[VMEM] * len(parts), out_specs=VMEM,
        out_shape=shape_of((len(parts) // 3,) + parts[0].shape, dtype),
        cost_estimate=SHORT, compiler_params=PARAMS,
    )(*parts)


def add_kernel(*refs):
    total = refs[0][...].astype(jnp.float32)
    for ref in refs[1:-1]:
        total = total + ref[...].astype(jnp.float32)
    refs[-1][...] = total.astype(refs[-1].dtype)


def add(parts):
    return pl.pallas_call(
        add_kernel, in_specs=[VMEM] * len(parts), out_specs=VMEM,
        out_shape=shape_of(parts[0].shape, parts[0].dtype), cost_estimate=SHORT, compiler_params=PARAMS,
    )(*parts)


def adam_update(weights, first, second, gradient):
    first = BETA_ONE * first + (1.0 - BETA_ONE) * gradient
    second = BETA_TWO * second + (1.0 - BETA_TWO) * gradient * gradient
    root = second * lax.rsqrt(second)
    weights = weights - INNER_RATE * (first / (root + EPSILON) + DECAY * weights)
    return weights, first, second


def inner_steps(anchor, first, second, own, got, here):
    weights, one, two = anchor[here], first[(0,) + here], second[(0,) + here]
    total, itself, ahead, back = own
    last = itself[here] + ahead[here].astype(jnp.float32) + back[here].astype(jnp.float32)
    for step, value in enumerate((total[(0,) + here], last)):
        gradient = value + got[(step,) + here].astype(jnp.float32)
        weights, one, two = adam_update(weights, one, two, gradient)
    return weights, one, two


def code_kernel(turn, spot, anchor, first, second, *refs):
    own, (got, scale, out) = refs[:4], refs[4:]
    half = out.shape[0]
    base = lax.rem(spot[2] + turn, CORES) * half

    @pl.loop(0, half, step=16, unroll=2)
    def _(r):
        rows = pl.ds(pl.multiple_of(base + r, 16), 16)
        for c in range(0, anchor.shape[1], 256):
            here = (rows, pl.ds(c, 256))
            delta = anchor[here] - inner_steps(anchor, first, second, own, got, here)[0]
            for block in range(2):
                at = c // 128 + block
                power = jnp.broadcast_to(scale[0, rows, at : at + 1], (16, 128))
                ones = jnp.ones_like(power)
                factor = jnp.left_shift(ones, -power).astype(jnp.float32)
                back = jnp.left_shift(ones, power + LOWEST).astype(jnp.float32) * 2.0**-LOWEST
                coded = delta[:, block * 128 : (block + 1) * 128] * factor
                coded = jnp.clip(coded, -CODE_LIMIT, CODE_LIMIT).astype(jnp.bfloat16)
                out[pl.ds(pl.multiple_of(r, 16), 16), pl.ds(at * 128, 128)] = (
                    coded.astype(jnp.float32) * back
                ).astype(jnp.bfloat16)


def code(turn, spot, anchor, first, second, own, got, exponents):
    rows, width = anchor.shape
    return pl.pallas_call(
        functools.partial(code_kernel, turn),
        in_specs=[SMEM] + [VMEM] * 9, out_specs=VMEM,
        out_shape=shape_of((rows // CORES, width), jnp.bfloat16),
        cost_estimate=SHORT, compiler_params=PARAMS,
    )(spot, anchor, first, second, *own, got, exponents)


def moment_kernel(anchor, first, second, *refs):
    own, (got, new_first, new_second) = refs[:4], refs[4:]

    @pl.loop(0, anchor.shape[0], step=16)
    def _(r):
        rows = pl.ds(pl.multiple_of(r, 16), 16)
        for c in range(0, anchor.shape[1], 256):
            here = (rows, pl.ds(c, 256))
            _, one, two = inner_steps(anchor, first, second, own, got, here)
            new_first[(0,) + here] = one
            new_second[(0,) + here] = two


def moments(anchor, first, second, own, got):
    out = shape_of(first.shape, first.dtype)
    return pl.pallas_call(
        moment_kernel, in_specs=[VMEM] * 8, out_specs=[VMEM] * 2, out_shape=[out] * 2,
        cost_estimate=SHORT, compiler_params=PARAMS,
    )(anchor, first, second, *own, got)


def pair_kernel(spot, ours, got, keep, send):
    rows = keep.shape[0]
    for turn, out in ((1, send), (0, keep)):
        at = pl.ds(pl.multiple_of(lax.rem(spot[3] + turn, 2) * rows, rows), rows)
        total = ours[at, :].astype(jnp.float32) + got[at, :].astype(jnp.float32)
        out[...] = total.astype(out.dtype)


def pair_sum(spot, ours, got):
    rows, width = ours.shape
    out = shape_of((rows // 2, width), ours.dtype)
    return pl.pallas_call(
        pair_kernel, in_specs=[SMEM, VMEM, VMEM], out_specs=[VMEM] * 2, out_shape=[out] * 2,
        cost_estimate=SHORT, compiler_params=PARAMS,
    )(spot, ours, got)


def swap(block, line, core):
    pairs = [
        (z * CORES + c, (z ^ line) * CORES + (c ^ core)) for z in range(LINE) for c in range(CORES)
    ]
    return lax.ppermute(block, "replica", pairs)


def outer_kernel(turns, spot, anchor, momentum, *refs):
    totals, (new_weights, new_momentum, weights, moving, sems) = refs[: len(turns)], refs[-5:]
    rows = totals[0].shape[0]
    stores = []
    for part, ((core, line), total) in enumerate(zip(turns, totals)):
        quarter = lax.rem(spot[2] + core, CORES) * 2 + lax.rem(spot[3] + line, 2)
        tile = rows // 2
        for r in range(0, rows, tile):
            here = pl.ds(pl.multiple_of(quarter * rows + r, tile), tile)
            average = total[r : r + tile, :].astype(jnp.float32) * (1.0 / (LINE * CORES))
            moved = MOMENTUM * momentum[here, :] + average
            moving[part, r : r + tile, :] = moved
            weights[part, r : r + tile, :] = anchor[here, :] - OUTER_RATE * (average + MOMENTUM * moved)
            for k, (held, out) in enumerate(((moving, new_momentum), (weights, new_weights))):
                store = pltpu.make_async_copy(
                    held.at[part, pl.ds(r, tile)], out.at[here], sems.at[k, part, r // tile]
                )
                store.start()
                stores.append(store)
    for store in stores:
        store.wait()


def outer_step(turns, spot, anchor, momentum, totals, outs=()):
    count, (rows, width) = len(turns), totals[0].shape
    return pl.pallas_call(
        functools.partial(outer_kernel, turns),
        in_specs=[SMEM] + [VMEM] * (2 + count) + [HBM] * len(outs),
        out_specs=[HBM] * 2,
        out_shape=[shape_of(anchor.shape, anchor.dtype)] * 2,
        scratch_shapes=[
            pltpu.VMEM((count, rows, width), jnp.float32),
            pltpu.VMEM((count, rows, width), jnp.float32),
            pltpu.SemaphoreType.DMA((2, count, 2)),
        ],
        input_output_aliases={3 + count + k: k for k in range(len(outs))},
        cost_estimate=SHORT,
        compiler_params=PARAMS,
    )(spot, anchor, momentum, *totals, *outs)


def on_device(
    anchor, first_moment, second_moment, outer_momentum, activations, cotangents, token_ids, exponents
):
    place = lax.axis_index("fsdp").astype(jnp.int32)
    z, x, y = place // PLANE, (place // NY) % NX, place % NY
    copy = lax.axis_index("replica").astype(jnp.int32)
    live = jnp.sum((token_ids[0] != 0).astype(jnp.int32), axis=1)
    spot = jnp.stack([x, y, copy % CORES, copy // CORES, z, live[0], live[1]])

    rings = ("y", "x")

    sent = [pack("y", 0, spot, cotangents, activations)]
    sent.append(pack("x", 1, spot, cotangents, activations))

    def gather(ahead, back, handed):
        ahead = [along(ring, block, 1) for ring, block in zip(rings, ahead)]
        back = [along(ring, block, -1) for ring, block in zip(rings, back)]
        on = [along(ring, block[-handed:], 1) for ring, block in zip(rings, ahead)]
        off = [along(ring, block[-handed:], -1) for ring, block in zip(rings, back)]
        return [[ahead[step], back[step], on[step], off[step]] for step in range(2)]

    def reduce(pieces):
        parts = []
        for ring, piece in zip(("x", "y"), pieces):
            low, high = opposite(piece)
            low, high = along(ring, low, 1), along(ring, high, -1)
            own = itself(piece)
            ahead, back = nearest(piece, low, after(high, own))
            parts.append([own, along(ring, ahead, 1), along(ring, back, -1)])
        return parts

    soon = gather([block[1] for block in sent], [block[2] for block in sent], 4)
    soon = [[sent[step][0]] + soon[step] for step in range(2)]
    theirs = totals(sum(reduce(soon), []), jnp.bfloat16)
    got = lax.ppermute(theirs, "fsdp", fsdp_shift(1, 0, 0))
    late = gather([block[3] for block in sent], [block[4] for block in sent], 2)
    parts = reduce([soon[step] + late[step] for step in range(2)])
    own = [totals(parts[0], jnp.float32)] + parts[1]

    state = anchor, first_moment, second_moment, own, got
    other = swap(code(1, spot, *state, exponents), 0, 1)
    keep = code(0, spot, *state, exponents)
    new_first, new_second = moments(*state[:4], after(got, other))
    kept, sent = pair_sum(spot, keep, other)
    total = add([kept, swap(sent, 1, 0)])
    total = add([after(total, new_first), swap(total, 2, 0)])
    across = swap(total, 0, 1)
    beside = swap(total, 1, 0)
    outs = outer_step([(0, 0)], spot, anchor, outer_momentum, [total])
    last = swap(after(beside, outs), 0, 1)
    outs = outer_step([(0, 1), (1, 0)], spot, anchor, outer_momentum, [beside, across], outs)
    new_weights, new_momentum = outer_step([(1, 1)], spot, anchor, outer_momentum, [last], outs)
    return new_weights, new_momentum, new_first, new_second


def solution(mesh):
    in_specs = (
        P("fsdp", None),
        P("replica", "fsdp", None),
        P("replica", "fsdp", None),
        P("fsdp", None),
        P("replica", None, "fsdp", None),
        P("replica", None, "fsdp", None),
        P("replica", None, "fsdp"),
        P("replica", "fsdp", None),
    )
    out_specs = (
        P("fsdp", None),
        P("fsdp", None),
        P("replica", "fsdp", None),
        P("replica", "fsdp", None),
    )
    return jax.shard_map(
        on_device, mesh=mesh, in_specs=in_specs, out_specs=out_specs, check_vma=False
    )
```
